32 devices in a mesh: dp: 4 (over y, x), dom: 8 (over z, core).
Axes of the slice: x: 2, y: 2, z: 4, core: 2. Of those that a mesh axis runs over, the one named last changes fastest.
Arguments:
- features: bfloat16 [4, 4096, 128], P('dp', 'dom'), may hold values from -6 to 6
- keep_masks: bfloat16 [4, 4, 4096], P('dp', None, 'dom'), may hold values from 0 to 1, as said below
- serve_ids: int32 [4, 8, 8, 1], P('dp', 'dom'), may hold values from 0 to 3, as said below
- col_slot: int32 [4, 32, 4], P('dp', 'dom'), may hold values from 0 to 11, as said below
- adj_blocks: bfloat16 [4, 32, 4, 128, 128], P('dp', 'dom'), may hold values from -0.25 to 0.25
- node_labels: int32 [4, 4096], P('dp', 'dom'), may hold values from 0 to 171
- labeled: int32 [4, 4096], P('dp', 'dom'), may hold values 0 or 1
- weight_in: bfloat16 [128, 1024], replicated, may hold values from -0.5 to 0.5
- bias_in: float32 [1024], replicated, may hold values from -3 to 3
- weight_out: bfloat16 [1024, 172], replicated, may hold values from -0.1875 to 0.1875
- bias_out: float32 [172], replicated, may hold values from -4 to 4
Outputs:
- grad_weight_in: float32 [128, 1024], replicated
- grad_bias_in: float32 [1024], replicated
- grad_weight_out: float32 [1024, 172], replicated
- grad_bias_out: float32 [172], replicated
The draws below stay inside these ranges and needn't reach their ends.
Inputs may be any that keep to these rules, and one draw needn't show every extreme that they name: `serve_ids`: for each batch, sending device and receiving device: 1 distinct own tile numbers of the sender. `col_slot`: slots below 8 name received tiles; within one device's row tiles every such slot is named exactly once and each own tile slot exactly 2 times. `keep_masks`: values are 0 or 1.
All inputs are finite; a program needn't handle non-finite values. No bound on the sum of `labeled` on one device may be relied on, other than what follows from the above.
Results may differ from the reference program's by a relative error of at most 0.0015.
Values may be sent and summed in bfloat16 or wider, within the bound.
No kernel may reach another device: no remote copies, remote signals or barrier semaphores. Data moves between devices by JAX's collectives and lax.ppermute only.
A program may use at most 64 MiB of HBM per device.

```python
import jax
import jax.numpy as jnp
from jax import lax

FEAT = 128
CLASSES = 172
HIDDEN_SIZE = 1024
TILE = 128
SAMPLES = 4
ORDER = 2
CAP = 1
LOCAL = 2
TILES_DEV = 4
NB = 4
NODE_DEV = 512
TILES = 32
NODES = 4096
NNZ = 4
N_DOM = 8


def draw_keep_masks(key, part):
    return jax.random.randint(key, (NB, SAMPLES, NODES), 0, 2).astype(jnp.float32).astype(jnp.bfloat16)


def draw_serve_ids(key, part):
    subkeys = jax.random.split(key, NB * N_DOM * N_DOM)

    def choose(subkey):
        return jax.random.permutation(subkey, TILES_DEV)[:CAP]
    chosen = jax.vmap(choose)(subkeys)
    return chosen.reshape(NB, N_DOM, N_DOM, CAP).astype(jnp.int32)


def draw_col_slot(key, part):
    remote = N_DOM * CAP
    slot_list = jnp.concatenate([jnp.arange(remote, dtype=jnp.int32), remote + jnp.repeat(jnp.arange(TILES_DEV, dtype=jnp.int32), LOCAL)])
    subkeys = jax.random.split(key, NB * N_DOM)

    def shuffle(subkey):
        return jax.random.permutation(subkey, slot_list)
    shuffled = jax.vmap(shuffle)(subkeys)
    return shuffled.reshape(NB, TILES, NNZ).astype(jnp.int32)


def plant(drawn, key, smallest, top_value):
    index_at = [jax.random.randint(jax.random.fold_in(key, axis), (), 0, length) for axis, length in enumerate(drawn.shape)]
    main_axis = drawn.shape.index(max(drawn.shape))
    next_to = index_at[:main_axis] + [(index_at[main_axis] + 1) % drawn.shape[main_axis]] + index_at[main_axis + 1:]
    return drawn.at[tuple(index_at)].set(smallest).at[tuple(next_to)].set(top_value)


def shard_levels(stream_key, dims, shards, least, high):
    loudness, own = 1.0, jax.random.fold_in(stream_key, 6)
    for axis_at, blocks in shards:
        draws = jnp.exp(jax.random.uniform(jax.random.fold_in(own, axis_at), (blocks,), jnp.float32, least / len(shards), high / len(shards)))
        loudness = loudness * jnp.repeat(draws, dims[axis_at] // blocks).reshape([-1 if axis == axis_at else 1 for axis in range(len(dims))])
    return loudness


def gaussian(rng, dims, spread, most, cuts=(), held_as=jnp.bfloat16):
    factor_of = shard_levels(rng, dims, cuts, -0.22, 0.18) if cuts else 1.0
    values = jax.random.normal(rng, dims, jnp.float32) * spread * factor_of
    return jnp.minimum(jnp.maximum(values, -most), most).astype(held_as)


def setup_inputs(seed: int = 0) -> dict:
    keys = jax.random.split(jax.random.key(seed), 12)
    features = gaussian(keys[0], (NB, NODES, FEAT), 1.0, 6.0, ((0, 4), (1, 8)))
    keep_masks = draw_keep_masks(jax.random.fold_in(keys[11], 71), 0)
    serve_ids = draw_serve_ids(jax.random.fold_in(keys[11], 71), 0)
    col_slot = draw_col_slot(jax.random.fold_in(keys[11], 71), 0)
    adj_blocks = gaussian(keys[4], (NB, TILES, NNZ, TILE, TILE), (TILE * NNZ) ** -0.5, 0.25, ((0, 4), (1, 8)))
    node_labels = plant(jax.random.randint(keys[5], (NB, NODES), 0, CLASSES), jax.random.fold_in(keys[5], 1), 0, CLASSES - 1).astype(jnp.int32)
    labeled = plant((jax.random.randint(keys[6], (NB, NODES), 0, 2) < 1).astype(jnp.int32), jax.random.fold_in(keys[6], 1), 0, 1)
    weight_in = gaussian(keys[7], (FEAT, HIDDEN_SIZE), FEAT ** -0.5, 0.5)
    bias_in = gaussian(keys[8], (HIDDEN_SIZE,), 0.5, 3.0, (), jnp.float32)
    weight_out = gaussian(keys[9], (HIDDEN_SIZE, CLASSES), HIDDEN_SIZE ** -0.5, 0.1875)
    bias_out = gaussian(keys[10], (CLASSES,), 1.0, 4.0, (), jnp.float32)
    return dict(features=features, keep_masks=keep_masks, serve_ids=serve_ids, col_slot=col_slot, adj_blocks=adj_blocks, node_labels=node_labels, labeled=labeled, weight_in=weight_in, bias_in=bias_in, weight_out=weight_out, bias_out=bias_out)


KEEP_RATE = 0.5


def column_tiles(serve_ids, col_slot):
    remote = N_DOM * CAP
    requester = (jnp.arange(TILES, dtype=jnp.int32) // TILES_DEV)[:, None]
    clipped = jnp.minimum(col_slot, remote - 1).astype(jnp.int32)
    sender = clipped // CAP
    which_one = clipped % CAP
    served = serve_ids[sender, requester, which_one]
    far_tile = sender * TILES_DEV + served
    near_tile = requester * TILES_DEV + (col_slot - remote)
    return jnp.where(col_slot < remote, far_tile, near_tile).astype(jnp.int32)


def propagate(current, adj_blocks, columns):
    def one_tile(pair):
        tile_blocks, tile_cols = pair
        picked = current[tile_cols].astype(jnp.float32)
        return jnp.einsum("jab,jsbf->saf", tile_blocks.astype(jnp.float32), picked)
    return lax.map(one_tile, (adj_blocks, columns))


def mlp_grads(xbar, node_labels, labeled, weight_in, bias_in, weight_out, bias_out, scale):
    row_tiles, samples, tile_size, feat_size = xbar.shape
    classes = weight_out.shape[1]
    node_rows = xbar.reshape(-1, feat_size)
    hidden_pre = jnp.dot(node_rows, weight_in, preferred_element_type=jnp.float32) + bias_in
    activation = jax.nn.silu(hidden_pre).astype(jnp.bfloat16)
    logits = jnp.dot(activation, weight_out, preferred_element_type=jnp.float32) + bias_out
    expo = jnp.exp(logits)
    prob = (expo / jnp.sum(expo, -1, keepdims=True)).reshape(row_tiles, samples, tile_size, classes)
    average = jnp.mean(prob, axis=1)
    squares = average * average
    sharp = squares / jnp.sum(squares, -1, keepdims=True)
    onehot = (node_labels.reshape(row_tiles, tile_size)[..., None] == jnp.arange(classes, dtype=jnp.int32)).astype(jnp.float32)
    used = labeled.reshape(row_tiles, 1, tile_size, 1).astype(jnp.float32)
    push = 2.0 * (prob - sharp[:, None])
    inner = jnp.sum(push * prob, -1, keepdims=True)
    dlogits = (used * (prob - onehot[:, None]) + prob * (push - inner)) * scale
    dlogits = dlogits.reshape(-1, classes)
    dlog_b = dlogits.astype(jnp.bfloat16)
    grad_weight_out = jnp.dot(activation.T, dlog_b, preferred_element_type=jnp.float32)
    grad_bias_out = jnp.sum(dlogits, 0)
    dact = jnp.dot(dlog_b, weight_out.T, preferred_element_type=jnp.float32)
    sigma = jax.nn.sigmoid(hidden_pre)
    dpre = dact * sigma * (1.0 + hidden_pre * (1.0 - sigma))
    grad_bias_in = jnp.sum(dpre, 0)
    grad_weight_in = jnp.dot(node_rows.T, dpre.astype(jnp.bfloat16), preferred_element_type=jnp.float32)
    return grad_weight_in, grad_bias_in, grad_weight_out, grad_bias_out


def reference(features, keep_masks, serve_ids, col_slot, adj_blocks, node_labels, labeled, weight_in, bias_in, weight_out, bias_out):
    scale = 1.0 / (SAMPLES * NODE_DEV)

    def one_batch(inputs):
        feats, masks_b, serve_b, slots_b, blocks_b, labels_b, labeled_b = inputs
        columns = column_tiles(serve_b, slots_b)
        own_tiles = feats.reshape(TILES, TILE, FEAT)
        mask_tiles = masks_b.reshape(SAMPLES, TILES, TILE).transpose(1, 0, 2)
        masked = mask_tiles[:, :, :, None] * own_tiles[:, None, :, :]
        total = masked.astype(jnp.float32)
        current = masked
        for step in range(ORDER):
            result = propagate(current, blocks_b, columns)
            total = total + result
            current = result.astype(jnp.bfloat16)
        xbar = (total * (1.0 / ((ORDER + 1) * KEEP_RATE))).astype(jnp.bfloat16)
        return mlp_grads(xbar, labels_b, labeled_b, weight_in, bias_in, weight_out, bias_out, scale)

    stacked = lax.map(one_batch, (features, keep_masks, serve_ids, col_slot, adj_blocks, node_labels, labeled))
    return (jnp.sum(stacked[0], 0), jnp.sum(stacked[1], 0), jnp.sum(stacked[2], 0), jnp.sum(stacked[3], 0))
```

```python
import functools

import jax
import jax.numpy as jnp
from jax import lax
from jax.experimental import pallas as pl
from jax.experimental.pallas import tpu as pltpu
from jax.sharding import PartitionSpec as P

ORDER = 2
KEEP_RATE = 0.5
XBAR_SCALE = 1.0 / ((ORDER + 1) * KEEP_RATE)
F32, BF16, I16, I32 = jnp.float32, jnp.bfloat16, jnp.int16, jnp.int32
VMEM_LIMIT = 50 * 1024 * 1024
SMEM = pl.BlockSpec(memory_space=pltpu.SMEM)
VMEM = pl.BlockSpec(memory_space=pltpu.VMEM)
CHUNK = 256
TAIL = 8


def call(kernel, outs, ins, scratch=(), n_smem=0):
    return pl.pallas_call(
        kernel,
        out_shape=outs,
        in_specs=[SMEM] * n_smem + [VMEM] * (len(ins) - n_smem),
        out_specs=jax.tree.map(lambda _: VMEM, outs),
        scratch_shapes=list(scratch),
        compiler_params=pltpu.CompilerParams(vmem_limit_bytes=VMEM_LIMIT),
    )(*ins)


def like(shape, dtype):
    return jax.ShapeDtypeStruct(shape, dtype)


def select_kernel(info, serve, feats, masks, *msgs):
    tile = feats.shape[1]
    samples = masks.shape[0]
    for k in range(1, len(msgs) + 1):
        t = serve[info[0] ^ k]
        out = msgs[k - 1]
        out[:tile, :] = feats[t]
        m = masks[:, pl.ds(pl.multiple_of(t * tile, tile), tile)]
        out[tile:, :] = jnp.concatenate([m, jnp.zeros((out.shape[0] - tile - samples, tile), BF16)], 0)


def pool_index(info, serve, slots, r, j, dom, nnz):
    q = slots[r * nnz + j]
    k = q ^ info[0]
    own = (dom - 1) + serve[info[0]]
    return jnp.where(q >= dom, q - 1, jnp.where(k == 0, own, k - 1))


def hop_rows(info, serve, slots, adj, pool, r, dom):
    nnz = adj.shape[1]
    lhs = jnp.concatenate([adj[r, j] for j in range(nnz)], 1)
    rhs = jnp.concatenate([pool[pool_index(info, serve, slots, r, j, dom, nnz)] for j in range(nnz)], 0)
    return jnp.dot(lhs, rhs, preferred_element_type=F32)


def hop1_kernel(dom, info, serve, slots, feats, masks, adj, *refs):
    msgs, (cur, total), outs, pool = refs[: dom - 1], refs[dom - 1 : dom + 1], refs[dom + 1 : -1], refs[-1]
    tiles, tile, feat = feats.shape
    samples = masks.shape[0]

    def put(at, f, m):
        cols = jnp.concatenate([m.astype(F32), jnp.zeros((8 - samples, tile), F32)], 0).T
        f = f.astype(F32)
        for s in range(samples):
            pool[at, :, s * feat : (s + 1) * feat] = (f * cols[:, s : s + 1]).astype(BF16)

    for k in range(dom - 1):
        put(k, msgs[k][:tile, :], msgs[k][tile : tile + samples, :])
    for t in range(tiles):
        put(dom - 1 + t, feats[t], masks[:, t * tile : (t + 1) * tile])
    for r in range(tiles):
        hop = hop_rows(info, serve, slots, adj, pool, r, dom)
        cur[r] = hop.astype(BF16)
        total[r] = hop + pool[dom - 1 + r].astype(F32)
    for k in range(1, dom):
        outs[k - 1][...] = cur[serve[info[0] ^ k]]


def mlp_kernel(dom, samples, classes, scale, info, serve, slots, adj, cur, total, code, w_in, b_in, w_out, w_out_t, b_out, *refs):
    recv = refs[: dom - 1]
    keep, send, pool, x_t, act, slope, dl, dl_t, dpre, acc, bias_acc, cls_acc = refs[dom - 1 :]
    tiles, tile, lanes = cur.shape
    feat = lanes // samples
    hidden = w_in.shape[1]
    wide = w_out.shape[1]
    rows = samples * tile
    nch = hidden // CHUNK
    for k in range(dom - 1):
        pool[k] = recv[k][...]
    for t in range(tiles):
        pool[dom - 1 + t] = cur[t]
    bias_acc[...] = jnp.zeros(bias_acc.shape, F32)
    cls_acc[...] = jnp.zeros(cls_acc.shape, F32)

    def one_tile(r, carry):
        hop = hop_rows(info, serve, slots, adj, pool, r, dom)
        xbar = ((total[r] + hop) * XBAR_SCALE).astype(BF16)
        base = pl.multiple_of(r * rows, rows)
        logits = []
        for s in range(samples):
            x = xbar[:, s * feat : (s + 1) * feat]
            x_t[:, pl.ds(base + s * tile, tile)] = x.T
            for n in range(nch):
                cols = slice(n * CHUNK, (n + 1) * CHUNK)
                pre = jnp.dot(x, w_in[:, cols], preferred_element_type=F32) + b_in[:, cols]
                den = 1.0 + jnp.exp(jnp.minimum(-pre, 87.0))
                g = pl.reciprocal(den, approx=True)
                g = g * (2.0 - den * g)
                silu = pre * g
                act[pl.ds(base + s * tile, tile), cols] = silu.astype(BF16)
                slope[s * tile : (s + 1) * tile, cols] = g + silu * (1.0 - g)
            logits.append(
                jnp.dot(act[pl.ds(base + s * tile, tile), :], w_out[...], preferred_element_type=F32) + b_out[...]
            )
        step = 32
        for c in range(0, tile, step):
            prob = []
            for s in range(samples):
                e = jnp.exp(logits[s][c : c + step])
                prob.append(e / jnp.sum(e, -1, keepdims=True))
            avg = sum(prob[1:], prob[0]) * (1.0 / samples)
            sq = avg * avg
            sharp = sq / jnp.sum(sq, -1, keepdims=True)
            label = code[r, c : c + step, :]
            hit = (lax.broadcasted_iota(I32, (step, wide), 1) == label).astype(F32)
            used = (label >= 0).astype(F32)
            part = jnp.zeros((step, wide), F32)
            for s in range(samples):
                p = prob[s]
                push = 2.0 * (p - sharp)
                inner = jnp.sum(push * p, -1, keepdims=True)
                d = (used * p - hit + p * (push - inner)) * scale
                part = part + d
                dl[s * tile + c : s * tile + c + step, :] = d.astype(BF16)
            cls_acc[...] += functools.reduce(lambda a, b: a + b, [part[i : i + 8] for i in range(0, step, 8)])
        for s in range(samples):
            d = dl[s * tile : (s + 1) * tile, :]
            dl_t[:, pl.ds(base + s * tile, tile)] = d.T[: dl_t.shape[0]]
            for n in range(nch):
                cols = slice(n * CHUNK, (n + 1) * CHUNK)
                dact = jnp.dot(d, w_out_t[:, cols], preferred_element_type=F32)
                dp = dact * slope[s * tile : (s + 1) * tile, cols]
                dpre[pl.ds(base + s * tile, tile), cols] = dp.astype(BF16)
                bias_acc[:, cols] += functools.reduce(lambda a, b: a + b, [dp[i : i + 8] for i in range(0, tile, 8)])
        return carry

    lax.fori_loop(0, tiles, one_tile, 0)
    lanes_out = acc.shape[2]
    wide_t = dl_t.shape[0]
    cls = jnp.sum(cls_acc[...], 0, keepdims=True)
    for n in range(nch):
        cols = slice(n * CHUNK, (n + 1) * CHUNK)
        g_in = jnp.dot(x_t[...], dpre[:, cols], preferred_element_type=F32)
        g_out = jnp.dot(dl_t[...], act[:, cols], preferred_element_type=F32)
        g_bias = jnp.sum(bias_acc[:, cols], 0, keepdims=True)
        for i in range(CHUNK // lanes_out):
            at = n * (CHUNK // lanes_out) + i
            part = slice(i * lanes_out, (i + 1) * lanes_out)
            acc[at, :feat, :] = g_in[:, part]
            acc[at, feat : feat + wide_t, :] = g_out[:, part]
            acc[at, feat + wide_t :, :] = jnp.concatenate(
                [g_bias[:, part]]
                + [cls[:, i * lanes_out : (i + 1) * lanes_out] for i in range(wide // lanes_out)]
                + [jnp.zeros((TAIL - 1 - wide // lanes_out, lanes_out), F32)],
                0,
            )
    for m in range(keep.shape[0]):
        pair = (info[1] ^ m) * 2
        keep[m] = acc[pair + info[2]]
        send[m] = acc[pair + 1 - info[2]]


def encode(x, feat, n_tail):
    body = x.shape[0] - TAIL
    parts = [x[:feat], x[feat:body]] + [x[body + i : body + i + 1] for i in range(n_tail)]
    ints, exps = [], []
    for p in parts:
        top = jnp.max(jnp.abs(p), 0, keepdims=True)
        e = jnp.floor(jnp.log2(jnp.maximum(top, 1e-30)))
        q = jnp.round(p * jnp.exp2(14.0 - e))
        ints.append(jnp.clip(q, -32767.0, 32767.0).astype(I32))
        exps.append(e.astype(I32))
    used = 2 * n_tail + 2
    last = ints[2:] + exps + [jnp.zeros((2 * TAIL - used, x.shape[1]), I32)]
    return jnp.concatenate(ints[:2] + [jnp.concatenate(last, 0)], 0).astype(I16)


def decode(ref, feat, n_tail):
    body = ref.shape[0] - 2 * TAIL
    v = ref[...].astype(I32).astype(F32)
    last = v[body:]
    scales = jnp.exp2(last[n_tail : 2 * n_tail + 2] - 14.0)
    tail = jnp.concatenate(
        [last[:n_tail] * scales[2:], jnp.zeros((TAIL - n_tail, v.shape[1]), F32)], 0
    )
    return jnp.concatenate([v[:feat] * scales[0:1], v[feat:body] * scales[1:2], tail], 0)


def pair_kernel(feat, n_tail, keep, recv, own, *msgs):
    own[...] = keep[0] + recv[0]
    for m in range(1, keep.shape[0]):
        msgs[m - 1][...] = encode(keep[m] + recv[m], feat, n_tail)


def scatter_kernel(feat, n_tail, own, *refs):
    total = own[...]
    for ref in refs[:-1]:
        total = total + decode(ref, feat, n_tail)
    refs[-1][...] = encode(total, feat, n_tail)


def tree_kernel(feat, n_tail, *refs):
    parts = [decode(ref, feat, n_tail) for ref in refs[:-1]]
    while len(parts) > 1:
        parts = [a + b for a, b in zip(parts[::2], parts[1::2])]
    refs[-1][...] = encode(parts[0], feat, n_tail)


def unpack_kernel(feat, n_tail, classes, info, *refs):
    pieces, (g_in, b_in, g_out, b_out) = refs[:-4], refs[-4:]
    lanes = pieces[0].shape[1]
    half = len(pieces) // 2
    body = pieces[0].shape[0] - 2 * TAIL
    for c in range(2):
        for m in range(half):
            at = (info[1] ^ m) * 2 + (info[2] ^ c)
            x = decode(pieces[c * half + m], feat, n_tail)
            where = pl.ds(pl.multiple_of(at * lanes, lanes), lanes)
            g_in[:, where] = x[:feat]
            g_out[:, where] = x[feat : feat + classes]
            b_in[:, where] = x[body : body + 1]

            @pl.when(at == 0)
            def _():
                for i in range(n_tail - 1):
                    b_out[:, i * lanes : (i + 1) * lanes] = x[body + 1 + i : body + 2 + i]


def xor_permute(x, axis, mask):
    return lax.ppermute(x, axis, [(i, i ^ mask) for i in range(lax.axis_size(axis))])


def bit_groups(axis, first):
    size, bit, groups = lax.axis_size(axis), first, []
    while (1 << bit) < size:
        groups.append([m << bit for m in (1, 2, 3) if (m << bit) < size])
        bit += 2
    return groups


def reduce_grads(keep, send, info, feat, n_tail, classes, hidden):
    count, rows, lanes = keep.shape
    coded = like((rows + TAIL, lanes), I16)
    recv = xor_permute(send, "dom", 1)
    own, *msgs = call(
        functools.partial(pair_kernel, feat, n_tail),
        [like((rows, lanes), F32)] + [coded] * (count - 1),
        [keep, recv],
    )
    msgs = [xor_permute(x, "dp", m + 1) for m, x in enumerate(msgs)]
    q = call(functools.partial(scatter_kernel, feat, n_tail), coded, [own] + msgs)
    for axis, groups in (("dom", bit_groups("dom", 1)), ("dp", bit_groups("dp", 2))):
        for masks in groups:
            got = [xor_permute(q, axis, m) for m in masks]
            q = call(functools.partial(tree_kernel, feat, n_tail), coded, [q] + got)
    pieces = [q] + [xor_permute(q, "dp", m) for m in range(1, count)]
    pieces = pieces + [xor_permute(x, "dom", 1) for x in pieces]
    return call(
        functools.partial(unpack_kernel, feat, n_tail, classes),
        [like((feat, hidden), F32), like((1, hidden), F32), like((classes, hidden), F32), like((1, (n_tail - 1) * lanes), F32)],
        [info] + pieces,
        n_smem=1,
    )


def per_device(
    features,
    keep_masks,
    serve_ids,
    col_slot,
    adj_blocks,
    node_labels,
    labeled,
    weight_in,
    bias_in,
    weight_out,
    bias_out,
):
    tiles, nnz = col_slot.shape[1:]
    tile = adj_blocks.shape[-1]
    feat = features.shape[-1]
    samples = keep_masks.shape[1]
    hidden, classes = weight_out.shape
    dom = lax.axis_size("dom")
    me = lax.axis_index("dom")
    info = jnp.stack([me, lax.axis_index("dp") & 3, me & 1]).astype(I32)
    serve = serve_ids.reshape(-1)
    slots = col_slot.reshape(-1)
    adj = adj_blocks[0]
    feats = features.reshape(tiles, tile, feat)
    masks = keep_masks[0]
    lanes = samples * feat
    wide = -(-classes // 128) * 128

    msgs = call(
        select_kernel, [like((tile + 16, feat), BF16)] * (dom - 1), [info, serve, feats, masks], n_smem=2
    )
    msgs = [xor_permute(x, "dom", k + 1) for k, x in enumerate(msgs)]
    cur, total, *outs = call(
        functools.partial(hop1_kernel, dom),
        [like((tiles, tile, lanes), BF16), like((tiles, tile, lanes), F32)] + [like((tile, lanes), BF16)] * (dom - 1),
        [info, serve, slots, feats, masks, adj] + msgs,
        [pltpu.VMEM((dom - 1 + tiles, tile, lanes), BF16)],
        n_smem=3,
    )
    outs = [xor_permute(x, "dom", k + 1) for k, x in enumerate(outs)]

    code = jnp.where(labeled != 0, node_labels, -1).reshape(tiles, tile, 1)
    w_out = jnp.pad(weight_out, ((0, 0), (0, wide - classes)))
    b_out = jnp.pad(bias_out, (0, wide - classes), constant_values=-1e30).reshape(1, wide)
    rows = samples * tile
    all_rows = rows * tiles
    wide_t = -(-classes // 16) * 16
    piece = (feat + wide_t + TAIL, 128)
    pieces = hidden // 128
    keep, send = call(
        functools.partial(mlp_kernel, dom, samples, classes, 1.0 / (samples * tiles * tile)),
        [like((pieces // 2,) + piece, F32)] * 2,
        [info, serve, slots, adj, cur, total, code, weight_in, bias_in.reshape(1, hidden), w_out, w_out.T, b_out] + outs,
        [
            pltpu.VMEM((dom - 1 + tiles, tile, lanes), BF16),
            pltpu.VMEM((feat, all_rows), BF16),
            pltpu.VMEM((all_rows, hidden), BF16),
            pltpu.VMEM((rows, hidden), F32),
            pltpu.VMEM((rows, wide), BF16),
            pltpu.VMEM((wide_t, all_rows), BF16),
            pltpu.VMEM((all_rows, hidden), BF16),
            pltpu.VMEM((pieces,) + piece, F32),
            pltpu.VMEM((8, hidden), F32),
            pltpu.VMEM((8, wide), F32),
        ],
        n_smem=3,
    )
    g_in, b_in, g_out, b_out = reduce_grads(keep, send, info, feat, 1 + wide // 128, classes, hidden)
    return g_in, b_in.reshape(hidden), g_out.T, b_out.reshape(-1)[:classes]


def solution(mesh):
    placed = (
        P("dp", "dom", None),
        P("dp", None, "dom"),
        P("dp", "dom", None, None),
        P("dp", "dom", None),
        P("dp", "dom", None, None, None),
        P("dp", "dom"),
        P("dp", "dom"),
        P(),
        P(),
        P(),
        P(),
    )
    return jax.shard_map(
        per_device, mesh=mesh, in_specs=placed, out_specs=(P(), P(), P(), P()), check_vma=False
    )
```

```python
import functools

import jax
import jax.numpy as jnp
from jax import lax
from jax.experimental import pallas as pl
from jax.experimental.pallas import tpu as pltpu
from jax.sharding import PartitionSpec as P

ORDER = 2
KEEP_RATE = 0.5
XBAR_SCALE = 1.0 / ((ORDER + 1) * KEEP_RATE)
F32, BF16, I16, I32 = jnp.float32, jnp.bfloat16, jnp.int16, jnp.int32
MIB = 1024 * 1024
SMEM = pl.BlockSpec(memory_space=pltpu.SMEM)
VMEM = pl.BlockSpec(memory_space=pltpu.VMEM)
HBM = pl.BlockSpec(memory_space=pltpu.HBM)
CHUNK = 256
TAIL = 8


def call(kernel, outs, ins, scratch=(), n_smem=0, n_hbm=0, vmem=8):
    return pl.pallas_call(
        kernel,
        out_shape=outs,
        in_specs=[SMEM] * n_smem + [HBM] * n_hbm + [VMEM] * (len(ins) - n_smem - n_hbm),
        out_specs=jax.tree.map(lambda _: VMEM, outs),
        scratch_shapes=list(scratch),
        compiler_params=pltpu.CompilerParams(vmem_limit_bytes=vmem * MIB),
    )(*ins)


def like(shape, dtype):
    return jax.ShapeDtypeStruct(shape, dtype)


def select_kernel(info, serve, feats, masks, *refs):
    msgs, (held, sem, mask_sem) = refs[:-3], refs[-3:]
    tile = feats.shape[1]
    samples = masks.shape[0]
    ids = [serve[info[0] ^ k] for k in range(1, len(msgs) + 1)]
    copy = pltpu.make_async_copy(masks, held, mask_sem)
    copy.start()
    copies = [
        pltpu.make_async_copy(feats.at[t], out.at[pl.ds(0, tile)], sem.at[i])
        for i, (t, out) in enumerate(zip(ids, msgs))
    ]
    for c in copies:
        c.start()
    copy.wait()
    for t, out in zip(ids, msgs):
        m = held[:, pl.ds(pl.multiple_of(t * tile, tile), tile)]
        out[tile:, :] = jnp.concatenate([m, jnp.zeros((out.shape[0] - tile - samples, tile), BF16)], 0)
    for c in copies:
        c.wait()


def pool_index(info, serve, slots, r, j, dom, nnz):
    q = slots[r * nnz + j]
    k = q ^ info[0]
    own = (dom - 1) + serve[info[0]]
    return jnp.where(q >= dom, q - 1, jnp.where(k == 0, own, k - 1))


def hop_rows(info, serve, slots, adj, pool, r, dom):
    nnz = adj.shape[1]
    lhs = jnp.concatenate([adj[r, j] for j in range(nnz)], 1)
    rhs = jnp.concatenate([pool[pool_index(info, serve, slots, r, j, dom, nnz)] for j in range(nnz)], 0)
    return jnp.dot(lhs, rhs, preferred_element_type=F32)


def hop1_kernel(dom, info, serve, slots, feats, masks, adj, *refs):
    msgs, (cur, total), outs, pool = refs[: dom - 1], refs[dom - 1 : dom + 1], refs[dom + 1 : -1], refs[-1]
    tiles, tile, feat = feats.shape
    samples = masks.shape[0]

    def put(at, f, m):
        cols = jnp.concatenate([m.astype(F32), jnp.zeros((8 - samples, tile), F32)], 0).T
        f = f.astype(F32)
        for s in range(samples):
            pool[at, :, s * feat : (s + 1) * feat] = (f * cols[:, s : s + 1]).astype(BF16)

    for k in range(dom - 1):
        put(k, msgs[k][:tile, :], msgs[k][tile : tile + samples, :])
    for t in range(tiles):
        put(dom - 1 + t, feats[t], masks[:, t * tile : (t + 1) * tile])
    for r in range(tiles):
        hop = hop_rows(info, serve, slots, adj, pool, r, dom)
        cur[r] = hop.astype(BF16)
        total[r] = hop + pool[dom - 1 + r].astype(F32)
    for k in range(1, dom):
        outs[k - 1][...] = cur[serve[info[0] ^ k]]


def mlp_kernel(dom, samples, classes, scale, info, serve, slots, adj, cur, total, code, w_in, b_in, w_out, w_out_t, b_out, *refs):
    recv = refs[: dom - 1]
    keep, send, pool, x_t, act, slope, dl, dl_t, dpre, acc, bias_acc, cls_acc = refs[dom - 1 :]
    tiles, tile, lanes = cur.shape
    feat = lanes // samples
    hidden = w_in.shape[1]
    wide = w_out.shape[1]
    rows = samples * tile
    nch = hidden // CHUNK
    for k in range(dom - 1):
        pool[k] = recv[k][...]
    for t in range(tiles):
        pool[dom - 1 + t] = cur[t]
    bias_acc[...] = jnp.zeros(bias_acc.shape, F32)
    cls_acc[...] = jnp.zeros(cls_acc.shape, F32)

    def one_tile(r, carry):
        hop = hop_rows(info, serve, slots, adj, pool, r, dom)
        xbar = ((total[r] + hop) * XBAR_SCALE).astype(BF16)
        base = pl.multiple_of(r * rows, rows)
        logits = []
        for s in range(samples):
            x = xbar[:, s * feat : (s + 1) * feat]
            x_t[:, pl.ds(base + s * tile, tile)] = x.T
            for n in range(nch):
                cols = slice(n * CHUNK, (n + 1) * CHUNK)
                pre = jnp.dot(x, w_in[:, cols], preferred_element_type=F32) + b_in[:, cols]
                den = 1.0 + jnp.exp(jnp.minimum(-pre, 87.0))
                g = pl.reciprocal(den, approx=True)
                g = g * (2.0 - den * g)
                silu = pre * g
                act[pl.ds(base + s * tile, tile), cols] = silu.astype(BF16)
                slope[s * tile : (s + 1) * tile, cols] = g + silu * (1.0 - g)
            logits.append(
                jnp.dot(act[pl.ds(base + s * tile, tile), :], w_out[...], preferred_element_type=F32) + b_out[...]
            )
        step = 32
        for c in range(0, tile, step):
            prob = []
            for s in range(samples):
                e = jnp.exp(logits[s][c : c + step])
                prob.append(e / jnp.sum(e, -1, keepdims=True))
            avg = sum(prob[1:], prob[0]) * (1.0 / samples)
            sq = avg * avg
            sharp = sq / jnp.sum(sq, -1, keepdims=True)
            label = code[r, c : c + step, :]
            hit = (lax.broadcasted_iota(I32, (step, wide), 1) == label).astype(F32)
            used = (label >= 0).astype(F32)
            part = jnp.zeros((step, wide), F32)
            for s in range(samples):
                p = prob[s]
                push = 2.0 * (p - sharp)
                inner = jnp.sum(push * p, -1, keepdims=True)
                d = (used * p - hit + p * (push - inner)) * scale
                part = part + d
                dl[s * tile + c : s * tile + c + step, :] = d.astype(BF16)
            cls_acc[...] += functools.reduce(lambda a, b: a + b, [part[i : i + 8] for i in range(0, step, 8)])
        for s in range(samples):
            d = dl[s * tile : (s + 1) * tile, :]
            dl_t[:, pl.ds(base + s * tile, tile)] = d.T[: dl_t.shape[0]]
            for n in range(nch):
                cols = slice(n * CHUNK, (n + 1) * CHUNK)
                dact = jnp.dot(d, w_out_t[:, cols], preferred_element_type=F32)
                dp = dact * slope[s * tile : (s + 1) * tile, cols]
                dpre[pl.ds(base + s * tile, tile), cols] = dp.astype(BF16)
                bias_acc[:, cols] += functools.reduce(lambda a, b: a + b, [dp[i : i + 8] for i in range(0, tile, 8)])
        return carry

    lax.fori_loop(0, tiles, one_tile, 0)
    lanes_out = acc.shape[2]
    wide_t = dl_t.shape[0]
    cls = jnp.sum(cls_acc[...], 0, keepdims=True)
    for n in range(nch):
        cols = slice(n * CHUNK, (n + 1) * CHUNK)
        g_in = jnp.dot(x_t[...], dpre[:, cols], preferred_element_type=F32)
        g_out = jnp.dot(dl_t[...], act[:, cols], preferred_element_type=F32)
        g_bias = jnp.sum(bias_acc[:, cols], 0, keepdims=True)
        for i in range(CHUNK // lanes_out):
            at = n * (CHUNK // lanes_out) + i
            part = slice(i * lanes_out, (i + 1) * lanes_out)
            acc[at, :feat, :] = g_in[:, part]
            acc[at, feat : feat + wide_t, :] = g_out[:, part]
            acc[at, feat + wide_t :, :] = jnp.concatenate(
                [g_bias[:, part]]
                + [cls[:, i * lanes_out : (i + 1) * lanes_out] for i in range(wide // lanes_out)]
                + [jnp.zeros((TAIL - 1 - wide // lanes_out, lanes_out), F32)],
                0,
            )
    for m in range(keep.shape[0]):
        pair = (info[1] ^ m) * 2
        keep[m] = acc[pair + info[2]]
        send[m] = acc[pair + 1 - info[2]]


def encode(x, feat, n_tail):
    body = x.shape[0] - TAIL
    parts = [x[:feat], x[feat:body]] + [x[body + i : body + i + 1] for i in range(n_tail)]
    ints, exps = [], []
    for p in parts:
        top = jnp.max(jnp.abs(p), 0, keepdims=True)
        e = jnp.floor(jnp.log2(jnp.maximum(top, 1e-30)))
        q = jnp.round(p * jnp.exp2(14.0 - e))
        ints.append(jnp.clip(q, -32767.0, 32767.0).astype(I32))
        exps.append(e.astype(I32))
    used = 2 * n_tail + 2
    last = ints[2:] + exps + [jnp.zeros((2 * TAIL - used, x.shape[1]), I32)]
    return jnp.concatenate(ints[:2] + [jnp.concatenate(last, 0)], 0).astype(I16)


def decode(ref, feat, n_tail):
    body = ref.shape[0] - 2 * TAIL
    v = ref[...].astype(I32).astype(F32)
    last = v[body:]
    scales = jnp.exp2(last[n_tail : 2 * n_tail + 2] - 14.0)
    tail = jnp.concatenate(
        [last[:n_tail] * scales[2:], jnp.zeros((TAIL - n_tail, v.shape[1]), F32)], 0
    )
    return jnp.concatenate([v[:feat] * scales[0:1], v[feat:body] * scales[1:2], tail], 0)


def pair_kernel(feat, n_tail, keep, recv, own, *msgs):
    own[...] = keep[0] + recv[0]
    for m in range(1, keep.shape[0]):
        msgs[m - 1][...] = encode(keep[m] + recv[m], feat, n_tail)


def scatter_kernel(feat, n_tail, own, *refs):
    total = own[...]
    for ref in refs[:-1]:
        total = total + decode(ref, feat, n_tail)
    refs[-1][...] = encode(total, feat, n_tail)


def tree_kernel(feat, n_tail, *refs):
    parts = [decode(ref, feat, n_tail) for ref in refs[:-1]]
    while len(parts) > 1:
        parts = [a + b for a, b in zip(parts[::2], parts[1::2])]
    refs[-1][...] = encode(parts[0], feat, n_tail)


def unpack_kernel(feat, n_tail, classes, info, *refs):
    pieces, (g_in, b_in, g_out, b_out) = refs[:-4], refs[-4:]
    lanes = pieces[0].shape[1]
    half = len(pieces) // 2
    body = pieces[0].shape[0] - 2 * TAIL
    for c in range(2):
        for m in range(half):
            at = (info[1] ^ m) * 2 + (info[2] ^ c)
            x = decode(pieces[c * half + m], feat, n_tail)
            where = pl.ds(pl.multiple_of(at * lanes, lanes), lanes)
            g_in[:, where] = x[:feat]
            g_out[:, where] = x[feat : feat + classes]
            b_in[:, where] = x[body : body + 1]

            @pl.when(at == 0)
            def _():
                for i in range(n_tail - 1):
                    b_out[:, i * lanes : (i + 1) * lanes] = x[body + 1 + i : body + 2 + i]


def xor_permute(x, axis, mask):
    return lax.ppermute(x, axis, [(i, i ^ mask) for i in range(lax.axis_size(axis))])


def swap_all(blocks):
    got = [xor_permute(blocks[k - 1], "dom", k) for k in range(len(blocks), 0, -1)]
    return got[::-1]


def bit_groups(axis, first):
    size, bit, groups = lax.axis_size(axis), first, []
    while (1 << bit) < size:
        groups.append([m << bit for m in (1, 2, 3) if (m << bit) < size])
        bit += 2
    return groups


def reduce_grads(keep, send, info, feat, n_tail, classes, hidden):
    count, rows, lanes = keep.shape
    coded = like((rows + TAIL, lanes), I16)
    recv = xor_permute(send, "dom", 1)
    own, *msgs = call(
        functools.partial(pair_kernel, feat, n_tail),
        [like((rows, lanes), F32)] + [coded] * (count - 1),
        [keep, recv],
    )
    msgs = [xor_permute(x, "dp", m + 1) for m, x in enumerate(msgs)]
    q = call(functools.partial(scatter_kernel, feat, n_tail), coded, [own] + msgs)
    for axis, groups in (("dom", bit_groups("dom", 1)), ("dp", bit_groups("dp", 2))):
        for masks in groups:
            got = [xor_permute(q, axis, m) for m in masks]
            q = call(functools.partial(tree_kernel, feat, n_tail), coded, [q] + got)
    pieces = [q] + [xor_permute(q, "dp", m) for m in range(1, count)]
    pieces = pieces + [xor_permute(x, "dom", 1) for x in pieces]
    return call(
        functools.partial(unpack_kernel, feat, n_tail, classes),
        [like((feat, hidden), F32), like((1, hidden), F32), like((classes, hidden), F32), like((1, (n_tail - 1) * lanes), F32)],
        [info] + pieces,
        n_smem=1,
    )


def per_device(
    features,
    keep_masks,
    serve_ids,
    col_slot,
    adj_blocks,
    node_labels,
    labeled,
    weight_in,
    bias_in,
    weight_out,
    bias_out,
):
    tiles, nnz = col_slot.shape[1:]
    tile = adj_blocks.shape[-1]
    feat = features.shape[-1]
    samples = keep_masks.shape[1]
    hidden, classes = weight_out.shape
    dom = lax.axis_size("dom")
    me = lax.axis_index("dom")
    info = jnp.stack([me, lax.axis_index("dp") & 3, me & 1]).astype(I32)
    serve = serve_ids.reshape(-1)
    slots = col_slot.reshape(-1)
    adj = adj_blocks[0]
    feats = features.reshape(tiles, tile, feat)
    masks = keep_masks[0]
    lanes = samples * feat
    wide = -(-classes // 128) * 128

    msgs = call(
        select_kernel,
        [like((tile + 16, feat), BF16)] * (dom - 1),
        [info, serve, feats, masks],
        [pltpu.VMEM(masks.shape, BF16), pltpu.SemaphoreType.DMA((dom - 1,)), pltpu.SemaphoreType.DMA],
        n_smem=2,
        n_hbm=2,
    )
    msgs = swap_all(msgs)
    cur, total, *outs = call(
        functools.partial(hop1_kernel, dom),
        [like((tiles, tile, lanes), BF16), like((tiles, tile, lanes), F32)] + [like((tile, lanes), BF16)] * (dom - 1),
        [info, serve, slots, feats, masks, adj] + msgs,
        [pltpu.VMEM((dom - 1 + tiles, tile, lanes), BF16)],
        n_smem=3,
    )
    outs = swap_all(outs)

    code = jnp.where(labeled != 0, node_labels, -1).reshape(tiles, tile, 1)
    w_out = jnp.pad(weight_out, ((0, 0), (0, wide - classes)))
    b_out = jnp.pad(bias_out, (0, wide - classes), constant_values=-1e30).reshape(1, wide)
    rows = samples * tile
    all_rows = rows * tiles
    wide_t = -(-classes // 16) * 16
    piece = (feat + wide_t + TAIL, 128)
    pieces = hidden // 128
    keep, send = call(
        functools.partial(mlp_kernel, dom, samples, classes, 1.0 / (samples * tiles * tile)),
        [like((pieces // 2,) + piece, F32)] * 2,
        [info, serve, slots, adj, cur, total, code, weight_in, bias_in.reshape(1, hidden), w_out, w_out.T, b_out] + outs,
        [
            pltpu.VMEM((dom - 1 + tiles, tile, lanes), BF16),
            pltpu.VMEM((feat, all_rows), BF16),
            pltpu.VMEM((all_rows, hidden), BF16),
            pltpu.VMEM((rows, hidden), F32),
            pltpu.VMEM((rows, wide), BF16),
            pltpu.VMEM((wide_t, all_rows), BF16),
            pltpu.VMEM((all_rows, hidden), BF16),
            pltpu.VMEM((pieces,) + piece, F32),
            pltpu.VMEM((8, hidden), F32),
            pltpu.VMEM((8, wide), F32),
        ],
        n_smem=3,
        vmem=28,
    )
    g_in, b_in, g_out, b_out = reduce_grads(keep, send, info, feat, 1 + wide // 128, classes, hidden)
    return g_in, b_in.reshape(hidden), g_out.T, b_out.reshape(-1)[:classes]


def solution(mesh):
    placed = (
        P("dp", "dom", None),
        P("dp", None, "dom"),
        P("dp", "dom", None, None),
        P("dp", "dom", None),
        P("dp", "dom", None, None, None),
        P("dp", "dom"),
        P("dp", "dom"),
        P(),
        P(),
        P(),
        P(),
    )
    return jax.shard_map(
        per_device, mesh=mesh, in_specs=placed, out_specs=(P(), P(), P(), P()), check_vma=False
    )
```

```python
import functools

import jax
import jax.numpy as jnp
from jax import lax
from jax.experimental import pallas as pl
from jax.experimental.pallas import tpu as pltpu
from jax.sharding import PartitionSpec as P

ORDER = 2
KEEP_RATE = 0.5
XBAR_SCALE = 1.0 / ((ORDER + 1) * KEEP_RATE)
F32, BF16, I16, I32 = jnp.float32, jnp.bfloat16, jnp.int16, jnp.int32
MIB = 1024 * 1024
SMEM = pl.BlockSpec(memory_space=pltpu.SMEM)
VMEM = pl.BlockSpec(memory_space=pltpu.VMEM)
HBM = pl.BlockSpec(memory_space=pltpu.HBM)
CHUNK = 256
BATCH = 1
TAIL = 8


def call(kernel, outs, ins, scratch=(), n_smem=0, n_hbm=0, vmem=8):
    return pl.pallas_call(
        kernel,
        out_shape=outs,
        in_specs=[SMEM] * n_smem + [HBM] * n_hbm + [VMEM] * (len(ins) - n_smem - n_hbm),
        out_specs=jax.tree.map(lambda _: VMEM, outs),
        scratch_shapes=list(scratch),
        compiler_params=pltpu.CompilerParams(vmem_limit_bytes=vmem * MIB),
    )(*ins)


def like(shape, dtype):
    return jax.ShapeDtypeStruct(shape, dtype)


def partners(dom):
    tops = [1 << b for b in reversed(range((dom - 1).bit_length()))]
    return [k for odd in (0, 1) for top in tops for k in range(top, 2 * top) if k % 2 == odd]


def select_kernel(info, feats, masks, *msgs):
    tile = feats.shape[1]
    samples = masks.shape[0]
    for i, k in enumerate(partners(len(msgs) + 1)):
        t = info[3 + (info[0] ^ k)]
        out = msgs[i]
        out[:tile, :] = feats[t]
        m = masks[:, pl.ds(pl.multiple_of(t * tile, tile), tile)]
        out[tile:, :] = jnp.concatenate([m, jnp.zeros((out.shape[0] - tile - samples, tile), BF16)], 0)


def masked_tile(f, m, put):
    samples, tile = m.shape
    cols = jnp.concatenate([m.astype(F32), jnp.zeros((8 - samples, tile), F32)], 0).T
    f = f.astype(F32)
    for s in range(samples):
        put(s, (f * cols[:, s : s + 1]).astype(BF16))


def layout_kernel(after, feats, masks, adj, lhs, own):
    tiles, tile, feat = feats.shape
    for t in range(tiles):
        lhs[t] = jnp.concatenate([adj[t, j] for j in range(adj.shape[1])], 1)

        def put(s, x):
            own[t, :, s * feat : (s + 1) * feat] = x

        masked_tile(feats[t], masks[:, t * tile : (t + 1) * tile], put)


def pool_index(info, slots, r, j, dom, nnz):
    q = slots[r * nnz + j]
    k = q ^ info[0]
    own = (dom - 1) + info[3 + info[0]]
    return jnp.where(q >= dom, q - 1, jnp.where(k == 0, own, k - 1))


def hop_rows(info, slots, lhs, pool, r, dom):
    nnz = lhs.shape[2] // lhs.shape[1]
    rhs = jnp.concatenate([pool[pool_index(info, slots, r, j, dom, nnz)] for j in range(nnz)], 0)
    return jnp.dot(lhs[r], rhs, preferred_element_type=F32)


def hop1_kernel(dom, samples, info, slots, lhs, own, *refs):
    msgs, (cur, total), outs, pool = refs[: dom - 1], refs[dom - 1 : dom + 1], refs[dom + 1 : -1], refs[-1]
    tiles, tile, lanes = own.shape
    feat = lanes // samples
    for i, k in enumerate(partners(dom)):

        def put(s, x):
            pool[k - 1, :, s * feat : (s + 1) * feat] = x

        masked_tile(msgs[i][:tile, :], msgs[i][tile : tile + samples, :], put)
    for t in range(tiles):
        pool[dom - 1 + t] = own[t]
    for r in range(tiles):
        hop = hop_rows(info, slots, lhs, pool, r, dom)
        cur[r] = hop.astype(BF16)
        total[r] = hop + own[r].astype(F32)
    for i, k in enumerate(partners(dom)):
        outs[i][...] = cur[info[3 + (info[0] ^ k)]]


def mlp_kernel(dom, samples, classes, scale, info, slots, lhs, cur, total, code, w_in, b_in, w_out, w_out_t, b_out, *refs):
    recv = refs[: dom - 1]
    keep, send, pool, x_t, act, slope, prob, dl, dl_t, dpre, acc, bias_acc, cls_acc = refs[dom - 1 :]
    tiles, tile, lanes = cur.shape
    feat = lanes // samples
    hidden = w_in.shape[1]
    wide = w_out.shape[1]
    rows = samples * tile
    nch = hidden // CHUNK
    for i, k in enumerate(partners(dom)):
        pool[k - 1] = recv[i][...]
    for t in range(tiles):
        pool[dom - 1 + t] = cur[t]
    bias_acc[...] = jnp.zeros(bias_acc.shape, F32)
    cls_acc[...] = jnp.zeros(cls_acc.shape, F32)

    def one_tile(r, carry):
        hop = hop_rows(info, slots, lhs, pool, r, dom)
        xbar = ((total[r] + hop) * XBAR_SCALE).astype(BF16)
        base = pl.multiple_of(r * rows, rows)
        for s in range(samples):
            x_t[:, pl.ds(base + s * tile, tile)] = xbar[:, s * feat : (s + 1) * feat].T
        for s in range(0, samples, BATCH):
            x = jnp.concatenate([xbar[:, i * feat : (i + 1) * feat] for i in range(s, s + BATCH)], 0)
            here = pl.ds(base + s * tile, BATCH * tile)
            there = slice(s * tile, (s + BATCH) * tile)
            for n in range(nch):
                cols = slice(n * CHUNK, (n + 1) * CHUNK)
                half = jnp.dot(x, w_in[:, cols], preferred_element_type=F32) + b_in[:, cols]
                t = jnp.tanh(half)
                up = 1.0 + t
                silu = half * up
                act[here, cols] = silu.astype(BF16)
                slope[there, cols] = up + silu * (1.0 - t)
            logits = jnp.dot(act[here, :], w_out[...], preferred_element_type=F32) + b_out[...]
            e = jnp.exp(logits)
            prob[there, :] = e * (1.0 / jnp.sum(e, -1, keepdims=True))
        step = 32
        for c in range(0, tile, step):
            probs = [prob[s * tile + c : s * tile + c + step, :] for s in range(samples)]
            avg = sum(probs[1:], probs[0]) * (1.0 / samples)
            sq = avg * avg
            sharp = sq * (1.0 / jnp.sum(sq, -1, keepdims=True))
            label = code[r, c : c + step, :]
            hit = jnp.where(lax.broadcasted_iota(I32, (step, wide), 1) == label, scale, 0.0)
            used = jnp.where(label >= 0, scale, 0.0)
            part = jnp.zeros((step, wide), F32)
            for s, p in enumerate(probs):
                off = p - sharp
                inner = jnp.sum(off * p, -1, keepdims=True)
                d = p * ((2.0 * scale) * (off - inner) + used) - hit
                part = part + d
                dl[s * tile + c : s * tile + c + step, :] = d.astype(BF16)
            cls_acc[...] += functools.reduce(lambda a, b: a + b, [part[i : i + 8] for i in range(0, step, 8)])
        for s in range(samples):
            d = dl[s * tile : (s + 1) * tile, :]
            dl_t[:, pl.ds(base + s * tile, tile)] = d.T[: dl_t.shape[0]]
            for n in range(nch):
                cols = slice(n * CHUNK, (n + 1) * CHUNK)
                dact = jnp.dot(d, w_out_t[:, cols], preferred_element_type=F32)
                dp = dact * slope[s * tile : (s + 1) * tile, cols]
                dpre[pl.ds(base + s * tile, tile), cols] = dp.astype(BF16)
                bias_acc[:, cols] += functools.reduce(lambda a, b: a + b, [dp[i : i + 8] for i in range(0, tile, 8)])
        return carry

    lax.fori_loop(0, tiles, one_tile, 0)
    lanes_out = acc.shape[2]
    wide_t = dl_t.shape[0]
    cls = jnp.sum(cls_acc[...], 0, keepdims=True)
    for n in range(nch):
        cols = slice(n * CHUNK, (n + 1) * CHUNK)
        g_in = jnp.dot(x_t[...], dpre[:, cols], preferred_element_type=F32)
        g_out = jnp.dot(dl_t[...], act[:, cols], preferred_element_type=F32)
        g_bias = jnp.sum(bias_acc[:, cols], 0, keepdims=True)
        for i in range(CHUNK // lanes_out):
            at = n * (CHUNK // lanes_out) + i
            part = slice(i * lanes_out, (i + 1) * lanes_out)
            acc[at, :feat, :] = g_in[:, part]
            acc[at, feat : feat + wide_t, :] = g_out[:, part]
            acc[at, feat + wide_t :, :] = jnp.concatenate(
                [g_bias[:, part]]
                + [cls[:, i * lanes_out : (i + 1) * lanes_out] for i in range(wide // lanes_out)]
                + [jnp.zeros((TAIL - 1 - wide // lanes_out, lanes_out), F32)],
                0,
            )
    for m in range(keep.shape[0]):
        pair = (info[1] ^ m) * 2
        keep[m] = acc[pair + info[2]]
        send[m] = acc[pair + 1 - info[2]]


def mlp_call(dom, samples, tiles, tile, feat, hidden, classes, wide, ins):
    lanes = samples * feat
    rows = samples * tile
    all_rows = rows * tiles
    wide_t = -(-classes // 16) * 16
    piece = (feat + wide_t + TAIL, 128)
    pieces = hidden // 128
    return call(
        functools.partial(mlp_kernel, dom, samples, classes, 1.0 / (samples * tiles * tile)),
        [like((pieces // 2,) + piece, F32)] * 2,
        list(ins),
        [
            pltpu.VMEM((dom - 1 + tiles, tile, lanes), BF16),
            pltpu.VMEM((feat, all_rows), BF16),
            pltpu.VMEM((all_rows, hidden), BF16),
            pltpu.VMEM((rows, hidden), F32),
            pltpu.VMEM((rows, wide), F32),
            pltpu.VMEM((rows, wide), BF16),
            pltpu.VMEM((wide_t, all_rows), BF16),
            pltpu.VMEM((all_rows, hidden), BF16),
            pltpu.VMEM((pieces,) + piece, F32),
            pltpu.VMEM((8, hidden), F32),
            pltpu.VMEM((8, wide), F32),
        ],
        n_smem=2,
        vmem=28,
    )


def encode(x, feat, n_tail):
    body = x.shape[0] - TAIL
    parts = [x[:feat], x[feat:body]] + [x[body + i : body + i + 1] for i in range(n_tail)]
    ints, exps = [], []
    for p in parts:
        top = jnp.max(jnp.abs(p), 0, keepdims=True)
        e = jnp.floor(jnp.log2(jnp.maximum(top, 1e-30)))
        q = jnp.round(p * jnp.exp2(14.0 - e))
        ints.append(jnp.clip(q, -32767.0, 32767.0).astype(I32))
        exps.append(e.astype(I32))
    used = 2 * n_tail + 2
    last = ints[2:] + exps + [jnp.zeros((2 * TAIL - used, x.shape[1]), I32)]
    return jnp.concatenate(ints[:2] + [jnp.concatenate(last, 0)], 0).astype(I16)


def decode(ref, feat, n_tail):
    body = ref.shape[0] - 2 * TAIL
    v = ref[...].astype(I32).astype(F32)
    last = v[body:]
    scales = jnp.exp2(last[n_tail : 2 * n_tail + 2] - 14.0)
    tail = jnp.concatenate(
        [last[:n_tail] * scales[2:], jnp.zeros((TAIL - n_tail, v.shape[1]), F32)], 0
    )
    return jnp.concatenate([v[:feat] * scales[0:1], v[feat:body] * scales[1:2], tail], 0)


def pair_kernel(feat, n_tail, keep, recv, own, *msgs):
    own[...] = keep[0] + recv[0]
    for m in range(1, keep.shape[0]):
        msgs[m - 1][...] = encode(keep[m] + recv[m], feat, n_tail)


def scatter_kernel(feat, n_tail, n_out, own, *refs):
    total = own[...]
    msgs, outs = refs[: -n_out], refs[-n_out:]
    for ref in msgs:
        total = total + decode(ref, feat, n_tail)
    q = encode(total, feat, n_tail)
    for ref in outs:
        ref[...] = q


def tree_kernel(feat, n_tail, order, *refs):
    n_in = len(order) + 1
    parts = [decode(refs[i], feat, n_tail) for i in [n_in - 1] + [order.index(m) for m in range(len(order))]]
    while len(parts) > 1:
        parts = [a + b for a, b in zip(parts[::2], parts[1::2])]
    q = encode(parts[0], feat, n_tail)
    for ref in refs[n_in:]:
        ref[...] = q


def unpack_kernel(feat, n_tail, classes, info, *refs):
    pieces, (g_in, b_in, g_out, b_out) = refs[:-4], refs[-4:]
    lanes = pieces[0].shape[1]
    half = len(pieces) // 2
    body = pieces[0].shape[0] - 2 * TAIL
    for c in range(2):
        for m in range(half):
            at = (info[1] ^ m) * 2 + (info[2] ^ c)
            x = decode(pieces[c * half + m], feat, n_tail)
            where = pl.ds(pl.multiple_of(at * lanes, lanes), lanes)
            g_in[:, where] = x[:feat]
            g_out[:, where] = x[feat : feat + classes]
            b_in[:, where] = x[body : body + 1]

            @pl.when(at == 0)
            def _():
                for i in range(n_tail - 1):
                    b_out[:, i * lanes : (i + 1) * lanes] = x[body + 1 + i : body + 2 + i]


def xor_permute(x, axis, mask):
    return lax.ppermute(x, axis, [(i, i ^ mask) for i in range(lax.axis_size(axis))])


def swap_all(blocks):
    return [xor_permute(x, "dom", k) for k, x in zip(partners(len(blocks) + 1), blocks)]


def bit_groups(axis, first):
    size, bit, groups = lax.axis_size(axis), first, []
    while (1 << bit) < size:
        groups.append([m << bit for m in (1, 2, 3) if (m << bit) < size])
        bit += 2
    return groups


def reduce_grads(keep, send, info, feat, n_tail, classes, hidden):
    count, rows, lanes = keep.shape
    coded = like((rows + TAIL, lanes), I16)
    recv = xor_permute(send, "dom", 1)
    own, *msgs = call(
        functools.partial(pair_kernel, feat, n_tail),
        [like((rows, lanes), F32)] + [coded] * (count - 1),
        [keep, recv],
    )
    msgs = [xor_permute(x, "dp", m + 1) for m, x in enumerate(msgs)]
    groups = [("dom", masks) for masks in bit_groups("dom", 1)] + [("dp", masks) for masks in bit_groups("dp", 2)]
    qs = call(functools.partial(scatter_kernel, feat, n_tail, 4), [coded] * 4, [own] + msgs)
    for axis, masks in groups:
        order = [m for m in (1, 2, 0) if m < len(masks)]
        got = [xor_permute(qs[i + 1], axis, masks[m]) for i, m in enumerate(order)]
        qs = call(functools.partial(tree_kernel, feat, n_tail, order), [coded] * 4, got + [qs[0]])
    pieces = [qs[0]] + [xor_permute(qs[m], "dp", m) for m in range(1, count)]
    pieces = pieces + [xor_permute(x, "dom", 1) for x in pieces]
    return call(
        functools.partial(unpack_kernel, feat, n_tail, classes),
        [like((feat, hidden), F32), like((1, hidden), F32), like((classes, hidden), F32), like((1, (n_tail - 1) * lanes), F32)],
        [info] + pieces,
        n_smem=1,
    )


def per_device(
    features,
    keep_masks,
    serve_ids,
    col_slot,
    adj_blocks,
    node_labels,
    labeled,
    weight_in,
    bias_in,
    weight_out,
    bias_out,
):
    tiles, nnz = col_slot.shape[1:]
    tile = adj_blocks.shape[-1]
    feat = features.shape[-1]
    samples = keep_masks.shape[1]
    hidden, classes = weight_out.shape
    dom = lax.axis_size("dom")
    me = lax.axis_index("dom")
    place = jnp.stack([me, lax.axis_index("dp") & 3, me & 1]).astype(I32)
    info = jnp.concatenate([place, serve_ids.reshape(-1)])
    slots = col_slot.reshape(-1)
    adj = adj_blocks[0]
    feats = features.reshape(tiles, tile, feat)
    masks = keep_masks[0]
    lanes = samples * feat
    wide = -(-classes // 128) * 128

    msgs = call(
        select_kernel,
        [like((tile + 16, feat), BF16)] * (dom - 1),
        [info, feats, masks],
        n_smem=1,
    )
    lhs, own = call(
        layout_kernel,
        [like((tiles, tile, nnz * tile), BF16), like((tiles, tile, lanes), BF16)],
        [msgs[-1], feats, masks, adj],
        n_hbm=1,
    )
    msgs = swap_all(msgs)
    cur, total, *outs = call(
        functools.partial(hop1_kernel, dom, samples),
        [like((tiles, tile, lanes), BF16), like((tiles, tile, lanes), F32)] + [like((tile, lanes), BF16)] * (dom - 1),
        [info, slots, lhs, own] + msgs,
        [pltpu.VMEM((dom - 1 + tiles, tile, lanes), BF16)],
        n_smem=2,
    )
    outs = swap_all(outs)

    code = jnp.where(labeled != 0, node_labels, -1).reshape(tiles, tile, 1)
    w_out = jnp.pad(weight_out, ((0, 0), (0, wide - classes)))
    b_out = jnp.pad(bias_out, (0, wide - classes), constant_values=-1e30).reshape(1, wide)
    keep, send = mlp_call(
        dom, samples, tiles, tile, feat, hidden, classes, wide,
        [info, slots, lhs, cur, total, code, 0.5 * weight_in, 0.5 * bias_in.reshape(1, hidden), w_out, 0.5 * w_out.T, b_out] + outs,
    )
    g_in, b_in, g_out, b_out = reduce_grads(keep, send, info, feat, 1 + wide // 128, classes, hidden)
    return g_in, b_in.reshape(hidden), g_out.T, b_out.reshape(-1)[:classes]


def solution(mesh):
    placed = (
        P("dp", "dom", None),
        P("dp", None, "dom"),
        P("dp", "dom", None, None),
        P("dp", "dom", None),
        P("dp", "dom", None, None, None),
        P("dp", "dom"),
        P("dp", "dom"),
        P(),
        P(),
        P(),
        P(),
    )
    return jax.shard_map(
        per_device, mesh=mesh, in_specs=placed, out_specs=(P(), P(), P(), P()), check_vma=False
    )
```

```python
import functools

import jax
import jax.numpy as jnp
from jax import lax
from jax.experimental import pallas as pl
from jax.experimental.pallas import tpu as pltpu
from jax.sharding import PartitionSpec as P

ORDER = 2
KEEP_RATE = 0.5
XBAR_SCALE = 1.0 / ((ORDER + 1) * KEEP_RATE)
F32, BF16, I16, I32 = jnp.float32, jnp.bfloat16, jnp.int16, jnp.int32
MIB = 1024 * 1024
SMEM = pl.BlockSpec(memory_space=pltpu.SMEM)
VMEM = pl.BlockSpec(memory_space=pltpu.VMEM)
CHUNK = 256
BATCH = 2
TAIL = 8


def call(kernel, outs, ins, scratch=(), n_smem=0, vmem=8):
    return pl.pallas_call(
        kernel,
        out_shape=outs,
        in_specs=[SMEM] * n_smem + [VMEM] * (len(ins) - n_smem),
        out_specs=jax.tree.map(lambda _: VMEM, outs),
        scratch_shapes=list(scratch),
        compiler_params=pltpu.CompilerParams(vmem_limit_bytes=vmem * MIB),
    )(*ins)


def like(shape, dtype):
    return jax.ShapeDtypeStruct(shape, dtype)


def partners(dom):
    tops = [1 << b for b in reversed(range((dom - 1).bit_length()))]
    return [k for odd in (0, 1) for top in tops for k in range(top, 2 * top) if k % 2 == odd]


def select_kernel(info, feats, masks, *refs):
    msgs = refs[:-2]
    refs[-2][...] = feats[...]
    refs[-1][...] = masks[...]
    tile = feats.shape[1]
    samples = masks.shape[0]
    for i, k in enumerate(partners(len(msgs) + 1)):
        t = info[3 + (info[0] ^ k)]
        out = msgs[i]
        out[:tile, :] = feats[t]
        m = masks[:, pl.ds(pl.multiple_of(t * tile, tile), tile)]
        out[tile:, :] = jnp.concatenate([m, jnp.zeros((out.shape[0] - tile - samples, tile), BF16)], 0)


def masked_tile(f, m, put):
    samples, tile = m.shape
    cols = jnp.concatenate([m.astype(F32), jnp.zeros((8 - samples, tile), F32)], 0).T
    f = f.astype(F32)
    for s in range(samples):
        put(s, (f * cols[:, s : s + 1]).astype(BF16))


def layout_kernel(feats, masks, adj, lhs, own):
    tiles, tile, feat = feats.shape
    for t in range(tiles):
        lhs[t] = jnp.concatenate([adj[t, j] for j in range(adj.shape[1])], 1)

        def put(s, x):
            own[t, :, s * feat : (s + 1) * feat] = x

        masked_tile(feats[t], masks[:, t * tile : (t + 1) * tile], put)


def pool_index(info, slots, r, j, dom, nnz):
    q = slots[r * nnz + j]
    k = q ^ info[0]
    own = (dom - 1) + info[3 + info[0]]
    return jnp.where(q >= dom, q - 1, jnp.where(k == 0, own, k - 1))


def hop_rows(info, slots, lhs, pool, r, dom):
    nnz = lhs.shape[2] // lhs.shape[1]
    rhs = jnp.concatenate([pool[pool_index(info, slots, r, j, dom, nnz)] for j in range(nnz)], 0)
    return jnp.dot(lhs[r], rhs, preferred_element_type=F32)


def hop1_kernel(dom, samples, info, slots, lhs, own, *refs):
    msgs, (cur, total), outs, pool = refs[: dom - 1], refs[dom - 1 : dom + 1], refs[dom + 1 : -1], refs[-1]
    tiles, tile, lanes = own.shape
    feat = lanes // samples
    for i, k in enumerate(partners(dom)):

        def put(s, x):
            pool[k - 1, :, s * feat : (s + 1) * feat] = x

        masked_tile(msgs[i][:tile, :], msgs[i][tile : tile + samples, :], put)
    for t in range(tiles):
        pool[dom - 1 + t] = own[t]
    for r in range(tiles):
        hop = hop_rows(info, slots, lhs, pool, r, dom)
        cur[r] = hop.astype(BF16)
        total[r] = hop + own[r].astype(F32)
    for i, k in enumerate(partners(dom)):
        outs[i][...] = cur[info[3 + (info[0] ^ k)]]


def fold(x):
    return functools.reduce(lambda a, b: a + b, [x[i : i + 8] for i in range(0, x.shape[0], 8)])


def mlp_kernel(dom, samples, scale, info, slots, lhs, cur, total, code, half_w, half_b, w_out, half_w_t, b_out, *refs):
    recv = refs[: dom - 1]
    send, x_t, act, dl_t, dpre, bias_acc, cls_acc, pool, slope, prob, dl = refs[dom - 1 :]
    tiles, tile, lanes = cur.shape
    feat = lanes // samples
    hidden = half_w.shape[1]
    wide = w_out.shape[1]
    rows = samples * tile
    nch = hidden // CHUNK
    for i, k in enumerate(partners(dom)):
        pool[k - 1] = recv[i][...]
    for t in range(tiles):
        pool[dom - 1 + t] = cur[t]
    bias_acc[...] = jnp.zeros(bias_acc.shape, F32)
    cls_acc[...] = jnp.zeros(cls_acc.shape, F32)

    def forward(r):
        hop = hop_rows(info, slots, lhs, pool, r, dom)
        xbar = ((total[r] + hop) * XBAR_SCALE).astype(BF16)
        base = r * rows
        for s in range(samples):
            x_t[:, base + s * tile : base + (s + 1) * tile] = xbar[:, s * feat : (s + 1) * feat].T
        batch = BATCH if samples % BATCH == 0 else 1
        for s in range(0, samples, batch):
            x = jnp.concatenate([xbar[:, i * feat : (i + 1) * feat] for i in range(s, s + batch)], 0)
            here = slice(base + s * tile, base + (s + batch) * tile)
            for n in range(nch):
                cols = slice(n * CHUNK, (n + 1) * CHUNK)
                h = jnp.dot(x, half_w[:, cols], preferred_element_type=F32) + half_b[:, cols]
                t = jnp.tanh(h)
                up = 1.0 + t
                silu = h * up
                act[here, cols] = silu.astype(BF16)
                slope[here, cols] = up + silu * (1.0 - t)
            logits = jnp.dot(act[here, :], w_out[...], preferred_element_type=F32) + b_out[...]
            e = jnp.exp(logits)
            prob[here, :] = e * (1.0 / jnp.sum(e, -1, keepdims=True))

    def backward(r):
        base = r * rows
        step = 32
        for c in range(0, tile, step):
            at = [slice(base + s * tile + c, base + s * tile + c + step) for s in range(samples)]
            probs = [prob[one, :] for one in at]
            avg = sum(probs[1:], probs[0]) * (1.0 / samples)
            sq = avg * avg
            sharp = sq * (1.0 / jnp.sum(sq, -1, keepdims=True))
            label = code[r, c : c + step, :]
            hit = jnp.where(lax.broadcasted_iota(I32, (step, wide), 1) == label, scale, 0.0)
            used = jnp.where(label >= 0, scale, 0.0)
            part = jnp.zeros((step, wide), F32)
            for one, p in zip(at, probs):
                off = p - sharp
                inner = jnp.sum(off * p, -1, keepdims=True)
                d = p * ((2.0 * scale) * (off - inner) + used) - hit
                part = part + d
                dl[one, :] = d.astype(BF16)
            cls_acc[...] += fold(part)
        for s in range(samples):
            here = slice(base + s * tile, base + (s + 1) * tile)
            d = dl[here, :]
            dl_t[:, here] = d.T[: dl_t.shape[0]]
            for n in range(nch):
                cols = slice(n * CHUNK, (n + 1) * CHUNK)
                dp = jnp.dot(d, half_w_t[:, cols], preferred_element_type=F32) * slope[here, cols]
                dpre[here, cols] = dp.astype(BF16)
                bias_acc[:, cols] += fold(dp)

    forward(0)
    for r in range(1, tiles):
        forward(r)
        backward(r - 1)
    backward(tiles - 1)
    half_pieces(1 - info[2], x_t, act, dl_t, dpre, bias_acc, cls_acc, lambda m: info[1] ^ m, send)


def half_pieces(core, x_t, act, dl_t, dpre, bias_acc, cls_acc, place, out):
    feat, wide_t = x_t.shape[0], dl_t.shape[0]
    half = act.shape[1] // 2
    wide = cls_acc.shape[1]
    lanes = out.shape[2]
    start = pl.multiple_of(core * half, half)
    chunk = min(CHUNK, half)
    each = chunk // lanes
    cls = jnp.sum(cls_acc[...], 0, keepdims=True)
    first = place(0)
    for n in range(half // chunk):
        cols = pl.ds(start + n * chunk, chunk)
        g_in = jnp.dot(x_t[...], dpre[:, cols], preferred_element_type=F32)
        g_out = jnp.dot(dl_t[...], act[:, cols], preferred_element_type=F32)
        g_bias = jnp.sum(bias_acc[:, cols], 0, keepdims=True)
        for i in range(each):
            at = (n * each + i) ^ first
            part = slice(i * lanes, (i + 1) * lanes)
            out[at, :feat, :] = g_in[:, part]
            out[at, feat : feat + wide_t, :] = g_out[:, part]
            out[at, feat + wide_t :, :] = jnp.concatenate(
                [g_bias[:, part]]
                + [cls[:, j * lanes : (j + 1) * lanes] for j in range(wide // lanes)]
                + [jnp.zeros((TAIL - 1 - wide // lanes, lanes), F32)],
                0,
            )


def keep_kernel(info, x_t, act, dl_t, dpre, bias_acc, cls_acc, keep):
    half_pieces(info[2], x_t, act, dl_t, dpre, bias_acc, cls_acc, lambda m: info[1] ^ m, keep)


def encode(x, feat, n_tail):
    body = x.shape[0] - TAIL
    parts = [x[:feat], x[feat:body]] + [x[body + i : body + i + 1] for i in range(n_tail)]
    ints, exps = [], []
    for p in parts:
        top = jnp.max(jnp.abs(p), 0, keepdims=True)
        e = jnp.floor(jnp.log2(jnp.maximum(top, 1e-30)))
        q = jnp.round(p * jnp.exp2(14.0 - e))
        ints.append(jnp.clip(q, -32767.0, 32767.0).astype(I32))
        exps.append(e.astype(I32))
    used = 2 * n_tail + 2
    last = ints[2:] + exps + [jnp.zeros((2 * TAIL - used, x.shape[1]), I32)]
    return jnp.concatenate(ints[:2] + [jnp.concatenate(last, 0)], 0).astype(I16)


def decode(ref, feat, n_tail):
    body = ref.shape[0] - 2 * TAIL
    v = ref[...].astype(I32).astype(F32)
    last = v[body:]
    scales = jnp.exp2(last[n_tail : 2 * n_tail + 2] - 14.0)
    tail = jnp.concatenate(
        [last[:n_tail] * scales[2:], jnp.zeros((TAIL - n_tail, v.shape[1]), F32)], 0
    )
    return jnp.concatenate([v[:feat] * scales[0:1], v[feat:body] * scales[1:2], tail], 0)


def pair_kernel(feat, n_tail, keep, recv, own, *msgs):
    own[...] = keep[0] + recv[0]
    for m in range(1, keep.shape[0]):
        msgs[m - 1][...] = encode(keep[m] + recv[m], feat, n_tail)


def scatter_kernel(feat, n_tail, n_out, own, *refs):
    total = own[...]
    msgs, outs = refs[: -n_out], refs[-n_out:]
    for ref in msgs:
        total = total + decode(ref, feat, n_tail)
    q = encode(total, feat, n_tail)
    for ref in outs:
        ref[...] = q


def tree_kernel(feat, n_tail, order, *refs):
    n_in = len(order) + 1
    parts = [decode(refs[i], feat, n_tail) for i in [n_in - 1] + [order.index(m) for m in range(len(order))]]
    while len(parts) > 1:
        parts = [a + b for a, b in zip(parts[::2], parts[1::2])]
    q = encode(parts[0], feat, n_tail)
    for ref in refs[n_in:]:
        ref[...] = q


def unpack_kernel(feat, n_tail, classes, info, *refs):
    pieces, (g_in, b_in, g_out, b_out) = refs[:-4], refs[-4:]
    lanes = pieces[0].shape[1]
    half = len(pieces) // 2
    body = pieces[0].shape[0] - 2 * TAIL
    for c in range(2):
        for m in range(half):
            at = (info[2] ^ c) * half + (info[1] ^ m)
            x = decode(pieces[c * half + m], feat, n_tail)
            where = pl.ds(pl.multiple_of(at * lanes, lanes), lanes)
            g_in[:, where] = x[:feat]
            g_out[:, where] = x[feat : feat + classes]
            b_in[:, where] = x[body : body + 1]

            @pl.when(at == 0)
            def _():
                for i in range(n_tail - 1):
                    b_out[:, i * lanes : (i + 1) * lanes] = x[body + 1 + i : body + 2 + i]


def xor_permute(x, axis, mask):
    return lax.ppermute(x, axis, [(i, i ^ mask) for i in range(lax.axis_size(axis))])


def swap_all(blocks):
    return [xor_permute(x, "dom", k) for k, x in zip(partners(len(blocks) + 1), blocks)]


def bit_groups(axis, first):
    size, bit, groups = lax.axis_size(axis), first, []
    while (1 << bit) < size:
        groups.append([m << bit for m in (1, 2, 3) if (m << bit) < size])
        bit += 2
    return groups


def reduce_grads(keep, recv, info, feat, n_tail, classes, hidden):
    count, rows, lanes = keep.shape
    coded = like((rows + TAIL, lanes), I16)
    own, *msgs = call(
        functools.partial(pair_kernel, feat, n_tail),
        [like((rows, lanes), F32)] + [coded] * (count - 1),
        [keep, recv],
    )
    msgs = [xor_permute(x, "dp", m + 1) for m, x in enumerate(msgs)]
    groups = [("dom", masks) for masks in bit_groups("dom", 1)] + [("dp", masks) for masks in bit_groups("dp", 2)]
    qs = call(functools.partial(scatter_kernel, feat, n_tail, 4), [coded] * 4, [own] + msgs)
    for axis, masks in groups:
        order = [m for m in (1, 2, 0) if m < len(masks)]
        got = [xor_permute(qs[i + 1], axis, masks[m]) for i, m in enumerate(order)]
        qs = call(functools.partial(tree_kernel, feat, n_tail, order), [coded] * 4, got + [qs[0]])
    pieces = [qs[0]] + [xor_permute(qs[m], "dp", m) for m in range(1, count)]
    pieces = pieces + [xor_permute(x, "dom", 1) for x in pieces]
    return call(
        functools.partial(unpack_kernel, feat, n_tail, classes),
        [like((feat, hidden), F32), like((1, hidden), F32), like((classes, hidden), F32), like((1, (n_tail - 1) * lanes), F32)],
        [info] + pieces,
        n_smem=1,
    )


def per_device(
    features,
    keep_masks,
    serve_ids,
    col_slot,
    adj_blocks,
    node_labels,
    labeled,
    weight_in,
    bias_in,
    weight_out,
    bias_out,
):
    tiles, nnz = col_slot.shape[1:]
    tile = adj_blocks.shape[-1]
    feat = features.shape[-1]
    samples = keep_masks.shape[1]
    hidden, classes = weight_out.shape
    dom = lax.axis_size("dom")
    me = lax.axis_index("dom")
    place = jnp.stack([me, lax.axis_index("dp") & 3, me & 1]).astype(I32)
    info = jnp.concatenate([place, serve_ids.reshape(-1)])
    slots = col_slot.reshape(-1)
    adj = adj_blocks[0]
    feats = features.reshape(tiles, tile, feat)
    masks = keep_masks[0]
    lanes = samples * feat
    wide = -(-classes // 128) * 128

    *msgs, feats, masks = call(
        select_kernel,
        [like((tile + 16, feat), BF16)] * (dom - 1) + [like(feats.shape, BF16), like(masks.shape, BF16)],
        [info, feats, masks],
        n_smem=1,
    )
    lhs, own = call(
        layout_kernel,
        [like((tiles, tile, nnz * tile), BF16), like((tiles, tile, lanes), BF16)],
        [feats, masks, adj],
    )
    msgs = swap_all(msgs)
    cur, total, *outs = call(
        functools.partial(hop1_kernel, dom, samples),
        [like((tiles, tile, lanes), BF16), like((tiles, tile, lanes), F32)] + [like((tile, lanes), BF16)] * (dom - 1),
        [info, slots, lhs, own] + msgs,
        [pltpu.VMEM((dom - 1 + tiles, tile, lanes), BF16)],
        n_smem=2,
    )
    outs = swap_all(outs)

    code = jnp.where(labeled != 0, node_labels, -1).reshape(tiles, tile, 1)
    w_out = jnp.pad(weight_out, ((0, 0), (0, wide - classes)))
    b_out = jnp.pad(bias_out, (0, wide - classes), constant_values=-1e30).reshape(1, wide)
    rows = samples * tile * tiles
    wide_t = -(-classes // 16) * 16
    half = like((hidden // 256, feat + wide_t + TAIL, 128), F32)
    send, *held = call(
        functools.partial(mlp_kernel, dom, samples, 1.0 / (samples * tiles * tile)),
        [
            half,
            like((feat, rows), BF16),
            like((rows, hidden), BF16),
            like((wide_t, rows), BF16),
            like((rows, hidden), BF16),
            like((8, hidden), F32),
            like((8, wide), F32),
        ],
        [info, slots, lhs, cur, total, code, 0.5 * weight_in, 0.5 * bias_in.reshape(1, hidden)]
        + [w_out, 0.5 * w_out.T, b_out]
        + outs,
        [
            pltpu.VMEM((dom - 1 + tiles, tile, lanes), BF16),
            pltpu.VMEM((rows, hidden), F32),
            pltpu.VMEM((rows, wide), F32),
            pltpu.VMEM((rows, wide), BF16),
        ],
        n_smem=2,
        vmem=24,
    )
    recv = xor_permute(send, "dom", 1)
    keep = call(keep_kernel, half, [info] + held, n_smem=1)
    g_in, b_in, g_out, b_out = reduce_grads(keep, recv, info, feat, 1 + wide // 128, classes, hidden)
    return g_in, b_in.reshape(hidden), g_out.T, b_out.reshape(-1)[:classes]


def solution(mesh):
    placed = (
        P("dp", "dom", None),
        P("dp", None, "dom"),
        P("dp", "dom", None, None),
        P("dp", "dom", None),
        P("dp", "dom", None, None, None),
        P("dp", "dom"),
        P("dp", "dom"),
        P(),
        P(),
        P(),
        P(),
    )
    return jax.shard_map(
        per_device, mesh=mesh, in_specs=placed, out_specs=(P(), P(), P(), P()), check_vma=False
    )
```

```python
import functools

import jax
import jax.numpy as jnp
from jax import lax
from jax.experimental import pallas as pl
from jax.experimental.pallas import tpu as pltpu
from jax.sharding import PartitionSpec as P

ORDER = 2
KEEP_RATE = 0.5
XBAR_SCALE = 1.0 / ((ORDER + 1) * KEEP_RATE)
F32, BF16, I16, I32 = jnp.float32, jnp.bfloat16, jnp.int16, jnp.int32
MIB = 1024 * 1024
SMEM = pl.BlockSpec(memory_space=pltpu.SMEM)
VMEM = pl.BlockSpec(memory_space=pltpu.VMEM)
CHUNK = 256
BATCH = 2
LATE = 4
TAIL = 8


def call(kernel, outs, ins, scratch=(), n_smem=0, vmem=8):
    return pl.pallas_call(
        kernel,
        out_shape=outs,
        in_specs=[SMEM] * n_smem + [VMEM] * (len(ins) - n_smem),
        out_specs=jax.tree.map(lambda _: VMEM, outs),
        scratch_shapes=list(scratch),
        compiler_params=pltpu.CompilerParams(vmem_limit_bytes=vmem * MIB),
    )(*ins)


def like(shape, dtype):
    return jax.ShapeDtypeStruct(shape, dtype)


def partners(dom):
    tops = [1 << b for b in reversed(range((dom - 1).bit_length()))]
    return [k for odd in (0, 1) for top in tops for k in range(top, 2 * top) if k % 2 == odd]


def select_kernel(info, feats, masks, *refs):
    msgs = refs[:-2]
    refs[-2][...] = feats[...]
    refs[-1][...] = masks[...]
    tile = feats.shape[1]
    samples = masks.shape[0]
    for i, k in enumerate(partners(len(msgs) + 1)):
        t = info[3 + (info[0] ^ k)]
        out = msgs[i]
        out[:tile, :] = feats[t]
        m = masks[:, pl.ds(pl.multiple_of(t * tile, tile), tile)]
        out[tile:, :] = jnp.concatenate([m, jnp.zeros((out.shape[0] - tile - samples, tile), BF16)], 0)


def masked_tile(f, m, put):
    samples, tile = m.shape
    cols = jnp.concatenate([m.astype(F32), jnp.zeros((8 - samples, tile), F32)], 0).T
    f = f.astype(F32)
    for s in range(samples):
        put(s, (f * cols[:, s : s + 1]).astype(BF16))


def layout_kernel(feats, masks, adj, slots, lhs, own, same_slots):
    same_slots[...] = slots[...]
    tiles, tile, feat = feats.shape
    for t in range(tiles):
        lhs[t] = jnp.concatenate([adj[t, j] for j in range(adj.shape[1])], 1)

        def put(s, x):
            own[t, :, s * feat : (s + 1) * feat] = x

        masked_tile(feats[t], masks[:, t * tile : (t + 1) * tile], put)


def pool_index(info, slots, r, j, dom, nnz):
    q = slots[r, j]
    k = q ^ info[0]
    own = (dom - 1) + info[3 + info[0]]
    return jnp.where(q >= dom, q - 1, jnp.where(k == 0, own, k - 1))


def hop_rows(info, slots, lhs, pool, r, dom):
    nnz = lhs.shape[2] // lhs.shape[1]
    rhs = jnp.concatenate([pool[pool_index(info, slots, r, j, dom, nnz)] for j in range(nnz)], 0)
    return jnp.dot(lhs[r], rhs, preferred_element_type=F32)


def hop1_kernel(dom, samples, info, slots, lhs, own, *refs):
    msgs, (cur, total), outs, pool = refs[: dom - 1], refs[dom - 1 : dom + 1], refs[dom + 1 : -1], refs[-1]
    tiles, tile, lanes = own.shape
    feat = lanes // samples
    for i, k in enumerate(partners(dom)):

        def put(s, x):
            pool[k - 1, :, s * feat : (s + 1) * feat] = x

        masked_tile(msgs[i][:tile, :], msgs[i][tile : tile + samples, :], put)
    for t in range(tiles):
        pool[dom - 1 + t] = own[t]
    for r in range(tiles):
        hop = hop_rows(info, slots, lhs, pool, r, dom)
        cur[r] = hop.astype(BF16)
        total[r] = hop + own[r].astype(F32)
    for i, k in enumerate(partners(dom)):
        outs[i][...] = cur[info[3 + (info[0] ^ k)]]


def fold(x):
    return functools.reduce(lambda a, b: a + b, [x[i : i + 8] for i in range(0, x.shape[0], 8)])


def prepare_kernel(
    w_in, b_in, w_out_t, b_out, labels, labeled, block, half_w, half_b, wide_w, half_w_t, wide_b, code, same_block
):
    same_block[...] = block[...]
    classes, hidden = w_out_t.shape
    wide = wide_w.shape[1]
    half_w[...] = w_in[...] * jnp.asarray(0.5, BF16)
    half_b[...] = b_in[...] * 0.5
    padded = jnp.concatenate([w_out_t[...], jnp.zeros((wide - classes, hidden), BF16)], 0)
    half_w_t[...] = padded * jnp.asarray(0.5, BF16)
    wide_w[...] = padded.T
    wide_b[...] = jnp.concatenate([b_out[...], jnp.full((1, wide - classes), -1e30, F32)], 1)
    tiles, tile = labels.shape
    rows = jnp.where(labeled[...] != 0, labels[...], -1).astype(F32)
    rows = jnp.concatenate([rows, jnp.zeros((-tiles % 8, tile), F32)], 0)
    code[...] = rows.T.astype(I32)


def mlp_kernel(dom, samples, scale, info, slots, lhs, cur, total, code, half_w, half_b, w_out, half_w_t, b_out, *refs):
    recv = refs[: dom - 1]
    send, x_t, act, dl_t, dpre, bias_acc, cls_acc, pool, slope, prob, dl = refs[dom - 1 :]
    tiles, tile, lanes = cur.shape
    feat = lanes // samples
    hidden = half_w.shape[1]
    wide = w_out.shape[1]
    rows = samples * tile
    nch = hidden // CHUNK
    for i, k in enumerate(partners(dom)):
        pool[k - 1] = recv[i][...]
    for t in range(tiles):
        pool[dom - 1 + t] = cur[t]
    bias_acc[...] = jnp.zeros(bias_acc.shape, F32)
    cls_acc[...] = jnp.zeros(cls_acc.shape, F32)

    def forward(r):
        hop = hop_rows(info, slots, lhs, pool, r, dom)
        xbar = ((total[r] + hop) * XBAR_SCALE).astype(BF16)
        base = r * rows
        for s in range(samples):
            x_t[:, base + s * tile : base + (s + 1) * tile] = xbar[:, s * feat : (s + 1) * feat].T
        batch = BATCH if samples % BATCH == 0 else 1
        for s in range(0, samples, batch):
            x = jnp.concatenate([xbar[:, i * feat : (i + 1) * feat] for i in range(s, s + batch)], 0)
            here = slice(base + s * tile, base + (s + batch) * tile)
            for n in range(nch):
                cols = slice(n * CHUNK, (n + 1) * CHUNK)
                h = jnp.dot(x, half_w[:, cols], preferred_element_type=F32) + half_b[:, cols]
                t = jnp.tanh(h)
                up = 1.0 + t
                silu = h * up
                act[here, cols] = silu.astype(BF16)
                slope[here, cols] = up + silu * (1.0 - t)
            logits = jnp.dot(act[here, :], w_out[...], preferred_element_type=F32) + b_out[...]
            e = jnp.exp(logits)
            prob[here, :] = e * (1.0 / jnp.sum(e, -1, keepdims=True))

    def backward(r):
        base = r * rows
        step = 32
        for c in range(0, tile, step):
            at = [slice(base + s * tile + c, base + s * tile + c + step) for s in range(samples)]
            probs = [prob[one, :] for one in at]
            avg = sum(probs[1:], probs[0]) * (1.0 / samples)
            sq = avg * avg
            sharp = sq * (1.0 / jnp.sum(sq, -1, keepdims=True))
            label = code[c : c + step, r : r + 1]
            hit = jnp.where(lax.broadcasted_iota(I32, (step, wide), 1) == label, scale, 0.0)
            used = jnp.where(label >= 0, scale, 0.0)
            part = jnp.zeros((step, wide), F32)
            for one, p in zip(at, probs):
                off = p - sharp
                inner = jnp.sum(off * p, -1, keepdims=True)
                d = p * ((2.0 * scale) * (off - inner) + used) - hit
                part = part + d
                dl[one, :] = d.astype(BF16)
            cls_acc[...] += fold(part)
        for s in range(samples):
            here = slice(base + s * tile, base + (s + 1) * tile)
            d = dl[here, :]
            dl_t[:, here] = d.T[: dl_t.shape[0]]
            for n in range(nch):
                cols = slice(n * CHUNK, (n + 1) * CHUNK)
                dp = jnp.dot(d, half_w_t[:, cols], preferred_element_type=F32) * slope[here, cols]
                dpre[here, cols] = dp.astype(BF16)
                bias_acc[:, cols] += fold(dp)

    forward(0)
    for r in range(1, tiles):
        forward(r)
        backward(r - 1)
    backward(tiles - 1)
    half_pieces(1 - info[2], x_t, act, dl_t, dpre, bias_acc, cls_acc, lambda m: info[1] ^ m, send)


def half_pieces(core, x_t, act, dl_t, dpre, bias_acc, cls_acc, place, out):
    feat, wide_t = x_t.shape[0], dl_t.shape[0]
    half = act.shape[1] // 2
    wide = cls_acc.shape[1]
    lanes = out.shape[2]
    start = pl.multiple_of(core * half, half)
    chunk = min(CHUNK, half)
    each = chunk // lanes
    cls = jnp.sum(cls_acc[...], 0, keepdims=True)
    first = place(0)
    for n in range(half // chunk):
        cols = pl.ds(start + n * chunk, chunk)
        g_in = jnp.dot(x_t[...], dpre[:, cols], preferred_element_type=F32)
        g_out = jnp.dot(dl_t[...], act[:, cols], preferred_element_type=F32)
        g_bias = jnp.sum(bias_acc[:, cols], 0, keepdims=True)
        for i in range(each):
            at = (n * each + i) ^ first
            part = slice(i * lanes, (i + 1) * lanes)
            out[at, :feat, :] = g_in[:, part]
            out[at, feat : feat + wide_t, :] = g_out[:, part]
            out[at, feat + wide_t :, :] = jnp.concatenate(
                [g_bias[:, part]]
                + [cls[:, j * lanes : (j + 1) * lanes] for j in range(wide // lanes)]
                + [jnp.zeros((TAIL - 1 - wide // lanes, lanes), F32)],
                0,
            )


def keep_kernel(info, x_t, act, dl_t, dpre, bias_acc, cls_acc, keep):
    half_pieces(info[2], x_t, act, dl_t, dpre, bias_acc, cls_acc, lambda m: info[1] ^ m, keep)


def encode(x, feat, n_tail):
    body = x.shape[0] - TAIL
    parts = [x[:feat], x[feat:body]] + [x[body + i : body + i + 1] for i in range(n_tail)]
    ints, exps = [], []
    for p in parts:
        top = jnp.max(jnp.abs(p), 0, keepdims=True)
        e = jnp.floor(jnp.log2(jnp.maximum(top, 1e-30)))
        q = jnp.round(p * jnp.exp2(14.0 - e))
        ints.append(jnp.clip(q, -32767.0, 32767.0).astype(I32))
        exps.append(e.astype(I32))
    used = 2 * n_tail + 2
    last = ints[2:] + exps + [jnp.zeros((2 * TAIL - used, x.shape[1]), I32)]
    return jnp.concatenate(ints[:2] + [jnp.concatenate(last, 0)], 0).astype(I16)


def decode(ref, feat, n_tail):
    body = ref.shape[0] - 2 * TAIL
    v = ref[...].astype(I32).astype(F32)
    last = v[body:]
    scales = jnp.exp2(last[n_tail : 2 * n_tail + 2] - 14.0)
    tail = jnp.concatenate(
        [last[:n_tail] * scales[2:], jnp.zeros((TAIL - n_tail, v.shape[1]), F32)], 0
    )
    return jnp.concatenate([v[:feat] * scales[0:1], v[feat:body] * scales[1:2], tail], 0)


def pair_kernel(feat, n_tail, keep, recv, own, *msgs):
    own[...] = keep[0] + recv[0]
    for m in range(1, keep.shape[0]):
        msgs[m - 1][...] = encode(keep[m] + recv[m], feat, n_tail)


def scatter_kernel(feat, n_tail, n_out, own, *refs):
    total = own[...]
    msgs, outs = refs[: -n_out], refs[-n_out:]
    for ref in msgs:
        total = total + decode(ref, feat, n_tail)
    q = encode(total, feat, n_tail)
    for ref in outs:
        ref[...] = q


def tree_kernel(feat, n_tail, order, *refs):
    n_in = len(order) + 1
    parts = [decode(refs[i], feat, n_tail) for i in [n_in - 1] + [order.index(m) for m in range(len(order))]]
    while len(parts) > 1:
        parts = [a + b for a, b in zip(parts[::2], parts[1::2])]
    q = encode(parts[0], feat, n_tail)
    for ref in refs[n_in:]:
        ref[...] = q


def unpack_kernel(feat, n_tail, classes, info, *refs):
    pieces, (g_in, b_in, g_out, b_out) = refs[:-4], refs[-4:]
    lanes = pieces[0].shape[1]
    half = len(pieces) // 2
    body = pieces[0].shape[0] - 2 * TAIL
    for c in range(2):
        for m in range(half):
            at = (info[2] ^ c) * half + (info[1] ^ m)
            x = decode(pieces[c * half + m], feat, n_tail)
            where = pl.ds(pl.multiple_of(at * lanes, lanes), lanes)
            g_in[:, where] = x[:feat]
            g_out[:, where] = x[feat : feat + classes]
            b_in[:, where] = x[body : body + 1]

            @pl.when(at == 0)
            def _():
                for i in range(n_tail - 1):
                    b_out[:, i * lanes : (i + 1) * lanes] = x[body + 1 + i : body + 2 + i]


def xor_permute(x, axis, mask):
    return lax.ppermute(x, axis, [(i, i ^ mask) for i in range(lax.axis_size(axis))])


def swap_all(blocks):
    return [xor_permute(x, "dom", k) for k, x in zip(partners(len(blocks) + 1), blocks)]


def bit_groups(axis, first):
    size, bit, groups = lax.axis_size(axis), first, []
    while (1 << bit) < size:
        groups.append([m << bit for m in (1, 2, 3) if (m << bit) < size])
        bit += 2
    return groups


def reduce_grads(keep, recv, info, feat, n_tail, classes, hidden):
    count, rows, lanes = keep.shape
    coded = like((rows + TAIL, lanes), I16)
    own, *msgs = call(
        functools.partial(pair_kernel, feat, n_tail),
        [like((rows, lanes), F32)] + [coded] * (count - 1),
        [keep, recv],
    )
    msgs = [xor_permute(x, "dp", m + 1) for m, x in enumerate(msgs)]
    groups = [("dom", masks) for masks in bit_groups("dom", 1)] + [("dp", masks) for masks in bit_groups("dp", 2)]
    qs = call(functools.partial(scatter_kernel, feat, n_tail, 4), [coded] * 4, [own] + msgs)
    for axis, masks in groups:
        order = [m for m in (1, 2, 0) if m < len(masks)]
        got = [xor_permute(qs[i + 1], axis, masks[m]) for i, m in enumerate(order)]
        qs = call(functools.partial(tree_kernel, feat, n_tail, order), [coded] * 4, got + [qs[0]])
    pieces = [qs[0]] + [xor_permute(qs[m], "dp", m) for m in range(1, count)]
    pieces = pieces + [xor_permute(x, "dom", 1) for x in pieces]
    return call(
        functools.partial(unpack_kernel, feat, n_tail, classes),
        [like((feat, hidden), F32), like((1, hidden), F32), like((classes, hidden), F32), like((1, (n_tail - 1) * lanes), F32)],
        [info] + pieces,
        n_smem=1,
    )


def per_device(
    features,
    keep_masks,
    serve_ids,
    col_slot,
    adj_blocks,
    node_labels,
    labeled,
    weight_in,
    bias_in,
    weight_out,
    bias_out,
):
    tiles, nnz = col_slot.shape[1:]
    tile = adj_blocks.shape[-1]
    feat = features.shape[-1]
    samples = keep_masks.shape[1]
    hidden, classes = weight_out.shape
    dom = lax.axis_size("dom")
    me = lax.axis_index("dom")
    place = jnp.stack([me, lax.axis_index("dp") & 3, me & 1]).astype(I32)
    info = jnp.concatenate([place, serve_ids.reshape(-1)])
    adj = adj_blocks[0]
    feats = features.reshape(tiles, tile, feat)
    masks = keep_masks[0]
    lanes = samples * feat
    wide = -(-classes // 128) * 128

    *msgs, feats, masks = call(
        select_kernel,
        [like((tile + 16, feat), BF16)] * (dom - 1) + [like(feats.shape, BF16), like(masks.shape, BF16)],
        [info, feats, masks],
        n_smem=1,
    )
    lhs, own, slots = call(
        layout_kernel,
        [like((tiles, tile, nnz * tile), BF16), like((tiles, tile, lanes), BF16), like((tiles, nnz), I32)],
        [feats, masks, adj, col_slot[0]],
    )
    msgs = swap_all(msgs)
    cur, total, *outs = call(
        functools.partial(hop1_kernel, dom, samples),
        [like((tiles, tile, lanes), BF16), like((tiles, tile, lanes), F32)] + [like((tile, lanes), BF16)] * (dom - 1),
        [info, slots, lhs, own] + msgs,
        [pltpu.VMEM((dom - 1 + tiles, tile, lanes), BF16)],
        n_smem=2,
    )
    late = min(LATE, dom - 2)
    half_w, half_b, w_out, half_w_t, b_out, code, outs[late] = call(
        prepare_kernel,
        [
            like((feat, hidden), BF16),
            like((1, hidden), F32),
            like((hidden, wide), BF16),
            like((wide, hidden), BF16),
            like((1, wide), F32),
            like((tile, -(-tiles // 8) * 8), I32),
            like(outs[late].shape, BF16),
        ],
        [weight_in, bias_in.reshape(1, hidden), weight_out.T, bias_out.reshape(1, classes)]
        + [node_labels.reshape(tiles, tile), labeled.reshape(tiles, tile), outs[late]],
    )
    outs = swap_all(outs)
    rows = samples * tile * tiles
    wide_t = -(-classes // 16) * 16
    half = like((hidden // 256, feat + wide_t + TAIL, 128), F32)
    send, *held = call(
        functools.partial(mlp_kernel, dom, samples, 1.0 / (samples * tiles * tile)),
        [
            half,
            like((feat, rows), BF16),
            like((rows, hidden), BF16),
            like((wide_t, rows), BF16),
            like((rows, hidden), BF16),
            like((8, hidden), F32),
            like((8, wide), F32),
        ],
        [info, slots, lhs, cur, total, code, half_w, half_b, w_out, half_w_t, b_out] + outs,
        [
            pltpu.VMEM((dom - 1 + tiles, tile, lanes), BF16),
            pltpu.VMEM((rows, hidden), F32),
            pltpu.VMEM((rows, wide), F32),
            pltpu.VMEM((rows, wide), BF16),
        ],
        n_smem=2,
        vmem=24,
    )
    recv = xor_permute(send, "dom", 1)
    keep = call(keep_kernel, half, [info] + held, n_smem=1)
    g_in, b_in, g_out, b_out = reduce_grads(keep, recv, info, feat, 1 + wide // 128, classes, hidden)
    return g_in, b_in.reshape(hidden), g_out.T, b_out.reshape(-1)[:classes]


def solution(mesh):
    placed = (
        P("dp", "dom", None),
        P("dp", None, "dom"),
        P("dp", "dom", None, None),
        P("dp", "dom", None),
        P("dp", "dom", None, None, None),
        P("dp", "dom"),
        P("dp", "dom"),
        P(),
        P(),
        P(),
        P(),
    )
    return jax.shard_map(
        per_device, mesh=mesh, in_specs=placed, out_specs=(P(), P(), P(), P()), check_vma=False
    )
```

```python
import functools

import jax
import jax.numpy as jnp
from jax import lax
from jax.experimental import pallas as pl
from jax.experimental.pallas import tpu as pltpu
from jax.sharding import PartitionSpec as P

ORDER = 2
KEEP_RATE = 0.5
XBAR_SCALE = 1.0 / ((ORDER + 1) * KEEP_RATE)
F32, BF16, I16, I32 = jnp.float32, jnp.bfloat16, jnp.int16, jnp.int32
MIB = 1024 * 1024
SMEM = pl.BlockSpec(memory_space=pltpu.SMEM)
VMEM = pl.BlockSpec(memory_space=pltpu.VMEM)
CHUNK = 256
BATCH = 2
LATE = 4
TAIL = 8


def call(kernel, outs, ins, scratch=(), n_smem=0, vmem=8):
    return pl.pallas_call(
        kernel,
        out_shape=outs,
        in_specs=[SMEM] * n_smem + [VMEM] * (len(ins) - n_smem),
        out_specs=jax.tree.map(lambda _: VMEM, outs),
        scratch_shapes=list(scratch),
        compiler_params=pltpu.CompilerParams(vmem_limit_bytes=vmem * MIB),
    )(*ins)


def like(shape, dtype):
    return jax.ShapeDtypeStruct(shape, dtype)


def partners(dom):
    tops = [1 << b for b in reversed(range((dom - 1).bit_length()))]
    return [k for odd in (0, 1) for top in tops for k in range(top, 2 * top) if k % 2 == odd]


def select_kernel(info, tiles, *refs):
    msgs = refs[:-1]
    refs[-1][...] = tiles[...]
    for i, k in enumerate(partners(len(msgs) + 1)):
        msgs[i][...] = tiles[info[3 + (info[0] ^ k)]]


def masked_tile(f, m, put):
    samples, tile = m.shape
    cols = jnp.concatenate([m.astype(F32), jnp.zeros((8 - samples, tile), F32)], 0).T
    f = f.astype(F32)
    for s in range(samples):
        put(s, (f * cols[:, s : s + 1]).astype(BF16))


def layout_kernel(samples, both, adj, slots, lhs, own, same_slots):
    same_slots[...] = slots[...]
    tiles, tile, lanes = own.shape
    feat = lanes // samples
    for t in range(tiles):
        lhs[t] = jnp.concatenate([adj[t, j] for j in range(adj.shape[1])], 1)

        def put(s, x):
            own[t, :, s * feat : (s + 1) * feat] = x

        masked_tile(both[t, :tile, :], both[t, tile : tile + samples, :], put)


def pool_index(info, slots, r, j, dom, nnz):
    q = slots[r, j]
    k = q ^ info[0]
    own = (dom - 1) + info[3 + info[0]]
    return jnp.where(q >= dom, q - 1, jnp.where(k == 0, own, k - 1))


def hop_rows(info, slots, lhs, pool, r, dom):
    nnz = lhs.shape[2] // lhs.shape[1]
    rhs = jnp.concatenate([pool[pool_index(info, slots, r, j, dom, nnz)] for j in range(nnz)], 0)
    return jnp.dot(lhs[r], rhs, preferred_element_type=F32)


def hop1_kernel(dom, samples, info, slots, lhs, own, *refs):
    msgs, (cur, total), outs, pool = refs[: dom - 1], refs[dom - 1 : dom + 1], refs[dom + 1 : -1], refs[-1]
    tiles, tile, lanes = own.shape
    feat = lanes // samples
    for i, k in enumerate(partners(dom)):

        def put(s, x):
            pool[k - 1, :, s * feat : (s + 1) * feat] = x

        masked_tile(msgs[i][:tile, :], msgs[i][tile : tile + samples, :], put)
    for t in range(tiles):
        pool[dom - 1 + t] = own[t]
    for r in range(tiles):
        hop = hop_rows(info, slots, lhs, pool, r, dom)
        cur[r] = hop.astype(BF16)
        total[r] = hop + own[r].astype(F32)
    for i, k in enumerate(partners(dom)):
        outs[i][...] = cur[info[3 + (info[0] ^ k)]]


def fold(x):
    return functools.reduce(lambda a, b: a + b, [x[i : i + 8] for i in range(0, x.shape[0], 8)])


def prepare_kernel(
    w_in, b_in, w_out_t, b_out, labels, labeled, block, half_w, half_b, wide_w, half_w_t, wide_b, code, same_block
):
    same_block[...] = block[...]
    classes, hidden = w_out_t.shape
    wide = wide_w.shape[1]
    half_w[...] = w_in[...] * jnp.asarray(0.5, BF16)
    half_b[...] = b_in[...] * 0.5
    padded = jnp.concatenate([w_out_t[...], jnp.zeros((wide - classes, hidden), BF16)], 0)
    half_w_t[...] = padded * jnp.asarray(0.5, BF16)
    wide_w[...] = padded.T
    wide_b[...] = jnp.concatenate([b_out[...], jnp.full((1, wide - classes), -1e30, F32)], 1)
    tiles, tile = labels.shape
    rows = jnp.where(labeled[...] != 0, labels[...], -1).astype(F32)
    rows = jnp.concatenate([rows, jnp.zeros((-tiles % 8, tile), F32)], 0)
    code[...] = rows.T.astype(I32)


def mlp_kernel(dom, samples, scale, info, slots, lhs, cur, total, code, half_w, half_b, w_out, half_w_t, b_out, *refs):
    recv = refs[: dom - 1]
    send, x_t, act, dl_t, dpre, bias_acc, cls_acc, pool, slope, prob, dl = refs[dom - 1 :]
    tiles, tile, lanes = cur.shape
    feat = lanes // samples
    hidden = half_w.shape[1]
    wide = w_out.shape[1]
    rows = samples * tile
    nch = hidden // CHUNK
    for i, k in enumerate(partners(dom)):
        pool[k - 1] = recv[i][...]
    for t in range(tiles):
        pool[dom - 1 + t] = cur[t]
    bias_acc[...] = jnp.zeros(bias_acc.shape, F32)
    cls_acc[...] = jnp.zeros(cls_acc.shape, F32)

    def forward(r):
        hop = hop_rows(info, slots, lhs, pool, r, dom)
        xbar = ((total[r] + hop) * XBAR_SCALE).astype(BF16)
        base = r * rows
        for s in range(samples):
            x_t[:, base + s * tile : base + (s + 1) * tile] = xbar[:, s * feat : (s + 1) * feat].T
        batch = BATCH if samples % BATCH == 0 else 1
        for s in range(0, samples, batch):
            x = jnp.concatenate([xbar[:, i * feat : (i + 1) * feat] for i in range(s, s + batch)], 0)
            here = slice(base + s * tile, base + (s + batch) * tile)
            for n in range(nch):
                cols = slice(n * CHUNK, (n + 1) * CHUNK)
                h = jnp.dot(x, half_w[:, cols], preferred_element_type=F32) + half_b[:, cols]
                t = jnp.tanh(h)
                up = 1.0 + t
                silu = h * up
                act[here, cols] = silu.astype(BF16)
                slope[here, cols] = up + silu * (1.0 - t)
            logits = jnp.dot(act[here, :], w_out[...], preferred_element_type=F32) + b_out[...]
            e = jnp.exp(logits)
            prob[here, :] = e * (1.0 / jnp.sum(e, -1, keepdims=True))

    def backward(r):
        base = r * rows
        step = 32
        for c in range(0, tile, step):
            at = [slice(base + s * tile + c, base + s * tile + c + step) for s in range(samples)]
            probs = [prob[one, :] for one in at]
            avg = sum(probs[1:], probs[0]) * (1.0 / samples)
            sq = avg * avg
            sharp = sq * (1.0 / jnp.sum(sq, -1, keepdims=True))
            label = code[c : c + step, r : r + 1]
            hit = jnp.where(lax.broadcasted_iota(I32, (step, wide), 1) == label, scale, 0.0)
            used = jnp.where(label >= 0, scale, 0.0)
            part = jnp.zeros((step, wide), F32)
            for one, p in zip(at, probs):
                off = p - sharp
                inner = jnp.sum(off * p, -1, keepdims=True)
                d = p * ((2.0 * scale) * (off - inner) + used) - hit
                part = part + d
                dl[one, :] = d.astype(BF16)
            cls_acc[...] += fold(part)
        for s in range(samples):
            here = slice(base + s * tile, base + (s + 1) * tile)
            d = dl[here, :]
            dl_t[:, here] = d.T[: dl_t.shape[0]]
            for n in range(nch):
                cols = slice(n * CHUNK, (n + 1) * CHUNK)
                dp = jnp.dot(d, half_w_t[:, cols], preferred_element_type=F32) * slope[here, cols]
                dpre[here, cols] = dp.astype(BF16)
                bias_acc[:, cols] += fold(dp)

    forward(0)
    for r in range(1, tiles):
        forward(r)
        backward(r - 1)
    backward(tiles - 1)
    half_pieces(1 - info[2], x_t, act, dl_t, dpre, bias_acc, cls_acc, lambda m: info[1] ^ m, send)


def half_pieces(core, x_t, act, dl_t, dpre, bias_acc, cls_acc, place, out):
    feat, wide_t = x_t.shape[0], dl_t.shape[0]
    half = act.shape[1] // 2
    wide = cls_acc.shape[1]
    lanes = out.shape[2]
    start = pl.multiple_of(core * half, half)
    chunk = min(CHUNK, half)
    each = chunk // lanes
    cls = jnp.sum(cls_acc[...], 0, keepdims=True)
    first = place(0)
    for n in range(half // chunk):
        cols = pl.ds(start + n * chunk, chunk)
        g_in = jnp.dot(x_t[...], dpre[:, cols], preferred_element_type=F32)
        g_out = jnp.dot(dl_t[...], act[:, cols], preferred_element_type=F32)
        g_bias = jnp.sum(bias_acc[:, cols], 0, keepdims=True)
        for i in range(each):
            at = (n * each + i) ^ first
            part = slice(i * lanes, (i + 1) * lanes)
            out[at, :feat, :] = g_in[:, part]
            out[at, feat : feat + wide_t, :] = g_out[:, part]
            out[at, feat + wide_t :, :] = jnp.concatenate(
                [g_bias[:, part]]
                + [cls[:, j * lanes : (j + 1) * lanes] for j in range(wide // lanes)]
                + [jnp.zeros((TAIL - 1 - wide // lanes, lanes), F32)],
                0,
            )


def keep_kernel(info, x_t, act, dl_t, dpre, bias_acc, cls_acc, keep):
    half_pieces(info[2], x_t, act, dl_t, dpre, bias_acc, cls_acc, lambda m: info[1] ^ m, keep)


def encode(x, feat, n_tail):
    body = x.shape[0] - TAIL
    parts = [x[:feat], x[feat:body]] + [x[body + i : body + i + 1] for i in range(n_tail)]
    ints, exps = [], []
    for p in parts:
        top = jnp.max(jnp.abs(p), 0, keepdims=True)
        e = jnp.floor(jnp.log2(jnp.maximum(top, 1e-30)))
        q = jnp.round(p * jnp.exp2(14.0 - e))
        ints.append(jnp.clip(q, -32767.0, 32767.0).astype(I32))
        exps.append(e.astype(I32))
    used = 2 * n_tail + 2
    last = ints[2:] + exps + [jnp.zeros((2 * TAIL - used, x.shape[1]), I32)]
    return jnp.concatenate(ints[:2] + [jnp.concatenate(last, 0)], 0).astype(I16)


def decode(ref, feat, n_tail):
    body = ref.shape[0] - 2 * TAIL
    v = ref[...].astype(I32).astype(F32)
    last = v[body:]
    scales = jnp.exp2(last[n_tail : 2 * n_tail + 2] - 14.0)
    tail = jnp.concatenate(
        [last[:n_tail] * scales[2:], jnp.zeros((TAIL - n_tail, v.shape[1]), F32)], 0
    )
    return jnp.concatenate([v[:feat] * scales[0:1], v[feat:body] * scales[1:2], tail], 0)


def pair_kernel(feat, n_tail, keep, recv, own, *msgs):
    own[...] = keep[0] + recv[0]
    for m in range(1, keep.shape[0]):
        msgs[m - 1][...] = encode(keep[m] + recv[m], feat, n_tail)


def scatter_kernel(feat, n_tail, n_out, own, *refs):
    total = own[...]
    msgs, outs = refs[: -n_out], refs[-n_out:]
    for ref in msgs:
        total = total + decode(ref, feat, n_tail)
    q = encode(total, feat, n_tail)
    for ref in outs:
        ref[...] = q


def tree_kernel(feat, n_tail, order, *refs):
    n_in = len(order) + 1
    parts = [decode(refs[i], feat, n_tail) for i in [n_in - 1] + [order.index(m) for m in range(len(order))]]
    while len(parts) > 1:
        parts = [a + b for a, b in zip(parts[::2], parts[1::2])]
    q = encode(parts[0], feat, n_tail)
    for ref in refs[n_in:]:
        ref[...] = q


def unpack_kernel(feat, n_tail, classes, info, *refs):
    pieces, (g_in, b_in, g_out, b_out) = refs[:-4], refs[-4:]
    lanes = pieces[0].shape[1]
    half = len(pieces) // 2
    body = pieces[0].shape[0] - 2 * TAIL
    for c in range(2):
        for i, m in enumerate((0,) + (3, 1, 2)):
            at = (info[2] ^ c) * half + (info[1] ^ m)
            x = decode(pieces[c * half + i], feat, n_tail)
            where = pl.ds(pl.multiple_of(at * lanes, lanes), lanes)
            g_in[:, where] = x[:feat]
            g_out[:, where] = x[feat : feat + classes]
            b_in[:, where] = x[body : body + 1]

            @pl.when(at == 0)
            def _():
                for j in range(n_tail - 1):
                    b_out[:, j * lanes : (j + 1) * lanes] = x[body + 1 + j : body + 2 + j]


def xor_permute(x, axis, mask):
    return lax.ppermute(x, axis, [(i, i ^ mask) for i in range(lax.axis_size(axis))])


def swap_all(blocks):
    return [xor_permute(x, "dom", k) for k, x in zip(partners(len(blocks) + 1), blocks)]


def bit_groups(axis, first):
    size, bit, groups = lax.axis_size(axis), first, []
    while (1 << bit) < size:
        groups.append([m << bit for m in (1, 2, 3) if (m << bit) < size])
        bit += 2
    return groups


def reduce_grads(keep, recv, info, feat, n_tail, classes, hidden):
    count, rows, lanes = keep.shape
    coded = like((rows + TAIL, lanes), I16)
    own, *msgs = call(
        functools.partial(pair_kernel, feat, n_tail),
        [like((rows, lanes), F32)] + [coded] * (count - 1),
        [keep, recv],
    )
    msgs = [xor_permute(x, "dp", m + 1) for m, x in enumerate(msgs)]
    groups = [("dom", masks) for masks in bit_groups("dom", 1)] + [("dp", masks) for masks in bit_groups("dp", 2)]
    qs = call(functools.partial(scatter_kernel, feat, n_tail, 4), [coded] * 4, [own] + msgs)
    for axis, masks in groups:
        order = [m for m in (1, 0, 2) if m < len(masks)]
        got = [xor_permute(qs[i + 1], axis, masks[m]) for i, m in enumerate(order)]
        qs = call(functools.partial(tree_kernel, feat, n_tail, order), [coded] * 4, got + [qs[0]])
    pieces = [qs[0]] + [xor_permute(qs[i + 1], "dp", m) for i, m in enumerate((3, 1, 2))]
    pieces = pieces + [xor_permute(x, "dom", 1) for x in pieces]
    return call(
        functools.partial(unpack_kernel, feat, n_tail, classes),
        [like((feat, hidden), F32), like((1, hidden), F32), like((classes, hidden), F32), like((1, (n_tail - 1) * lanes), F32)],
        [info] + pieces,
        n_smem=1,
    )


def per_device(
    features,
    keep_masks,
    serve_ids,
    col_slot,
    adj_blocks,
    node_labels,
    labeled,
    weight_in,
    bias_in,
    weight_out,
    bias_out,
):
    tiles, nnz = col_slot.shape[1:]
    tile = adj_blocks.shape[-1]
    feat = features.shape[-1]
    samples = keep_masks.shape[1]
    hidden, classes = weight_out.shape
    dom = lax.axis_size("dom")
    me = lax.axis_index("dom")
    place = jnp.stack([me, lax.axis_index("dp") & 3, me & 1]).astype(I32)
    info = jnp.concatenate([place, serve_ids.reshape(-1)])
    adj = adj_blocks[0]
    feats = features.reshape(tiles, tile, feat)
    masks = keep_masks[0]
    lanes = samples * feat
    wide = -(-classes // 128) * 128

    rows = jnp.pad(masks.reshape(samples, tiles, tile).transpose(1, 0, 2), ((0, 0), (0, 16 - samples), (0, 0)))
    both = jnp.concatenate([feats, rows], 1)
    *msgs, both = call(
        select_kernel, [like((tile + 16, feat), BF16)] * (dom - 1) + [like(both.shape, BF16)], [info, both], n_smem=1
    )
    lhs, own, slots = call(
        functools.partial(layout_kernel, samples),
        [like((tiles, tile, nnz * tile), BF16), like((tiles, tile, lanes), BF16), like((tiles, nnz), I32)],
        [both, adj, col_slot[0]],
    )
    msgs = swap_all(msgs)
    cur, total, *outs = call(
        functools.partial(hop1_kernel, dom, samples),
        [like((tiles, tile, lanes), BF16), like((tiles, tile, lanes), F32)] + [like((tile, lanes), BF16)] * (dom - 1),
        [info, slots, lhs, own] + msgs,
        [pltpu.VMEM((dom - 1 + tiles, tile, lanes), BF16)],
        n_smem=2,
    )
    late = min(LATE, dom - 2)
    half_w, half_b, w_out, half_w_t, b_out, code, outs[late] = call(
        prepare_kernel,
        [
            like((feat, hidden), BF16),
            like((1, hidden), F32),
            like((hidden, wide), BF16),
            like((wide, hidden), BF16),
            like((1, wide), F32),
            like((tile, -(-tiles // 8) * 8), I32),
            like(outs[late].shape, BF16),
        ],
        [weight_in, bias_in.reshape(1, hidden), weight_out.T, bias_out.reshape(1, classes)]
        + [node_labels.reshape(tiles, tile), labeled.reshape(tiles, tile), outs[late]],
    )
    outs = swap_all(outs)
    rows = samples * tile * tiles
    wide_t = -(-classes // 16) * 16
    half = like((hidden // 256, feat + wide_t + TAIL, 128), F32)
    send, *held = call(
        functools.partial(mlp_kernel, dom, samples, 1.0 / (samples * tiles * tile)),
        [
            half,
            like((feat, rows), BF16),
            like((rows, hidden), BF16),
            like((wide_t, rows), BF16),
            like((rows, hidden), BF16),
            like((8, hidden), F32),
            like((8, wide), F32),
        ],
        [info, slots, lhs, cur, total, code, half_w, half_b, w_out, half_w_t, b_out] + outs,
        [
            pltpu.VMEM((dom - 1 + tiles, tile, lanes), BF16),
            pltpu.VMEM((rows, hidden), F32),
            pltpu.VMEM((rows, wide), F32),
            pltpu.VMEM((rows, wide), BF16),
        ],
        n_smem=2,
        vmem=24,
    )
    recv = xor_permute(send, "dom", 1)
    keep = call(keep_kernel, half, [info] + held, n_smem=1)
    g_in, b_in, g_out, b_out = reduce_grads(keep, recv, info, feat, 1 + wide // 128, classes, hidden)
    return g_in, b_in.reshape(hidden), g_out.T, b_out.reshape(-1)[:classes]


def solution(mesh):
    placed = (
        P("dp", "dom", None),
        P("dp", None, "dom"),
        P("dp", "dom", None, None),
        P("dp", "dom", None),
        P("dp", "dom", None, None, None),
        P("dp", "dom"),
        P("dp", "dom"),
        P(),
        P(),
        P(),
        P(),
    )
    return jax.shard_map(
        per_device, mesh=mesh, in_specs=placed, out_specs=(P(), P(), P(), P()), check_vma=False
    )
```

```python
import functools

import jax
import jax.numpy as jnp
from jax import lax
from jax.experimental import pallas as pl
from jax.experimental.pallas import tpu as pltpu
from jax.sharding import PartitionSpec as P

ORDER = 2
KEEP_RATE = 0.5
XBAR_SCALE = 1.0 / ((ORDER + 1) * KEEP_RATE)
F32, BF16, I16, I32 = jnp.float32, jnp.bfloat16, jnp.int16, jnp.int32
MIB = 1024 * 1024
SMEM = pl.BlockSpec(memory_space=pltpu.SMEM)
VMEM = pl.BlockSpec(memory_space=pltpu.VMEM)
CHUNK = 256
AHEAD = 2
BATCH = 4
LATE = 4
TAIL = 8


def call(kernel, outs, ins, scratch=(), n_smem=0, vmem=8):
    return pl.pallas_call(
        kernel,
        out_shape=outs,
        in_specs=[SMEM] * n_smem + [VMEM] * (len(ins) - n_smem),
        out_specs=jax.tree.map(lambda _: VMEM, outs),
        scratch_shapes=list(scratch),
        compiler_params=pltpu.CompilerParams(vmem_limit_bytes=vmem * MIB),
    )(*ins)


def like(shape, dtype):
    return jax.ShapeDtypeStruct(shape, dtype)


def tops(dom):
    return [1 << b for b in reversed(range((dom - 1).bit_length()))]


def partners(dom):
    return [k for odd in (0, 1) for top in tops(dom) for k in range(top, 2 * top) if k % 2 == odd]


def partners_1(dom):
    return [k for top in tops(dom) for odd in (0, 1) for k in range(top, 2 * top) if k % 2 == odd]


def select_kernel(info, tiles, *refs):
    msgs = refs[:-1]
    refs[-1][...] = tiles[...]
    for i, k in enumerate(partners_1(len(msgs) + 1)):
        msgs[i][...] = tiles[info[3 + (info[0] ^ k)]]


def masked_tile(f, m, put):
    samples, tile = m.shape
    cols = jnp.concatenate([m.astype(F32), jnp.zeros((8 - samples, tile), F32)], 0).T
    f = f.astype(F32)
    for s in range(samples):
        put(s, (f * cols[:, s : s + 1]).astype(BF16))


def layout_kernel(samples, both, adj, slots, lhs, own, same_slots):
    same_slots[...] = slots[...]
    tiles, tile, lanes = own.shape
    feat = lanes // samples
    for t in range(tiles):
        lhs[t] = jnp.concatenate([adj[t, j] for j in range(adj.shape[1])], 1)

        def put(s, x):
            own[t, :, s * feat : (s + 1) * feat] = x

        masked_tile(both[t, :tile, :], both[t, tile : tile + samples, :], put)


def pool_index(info, slots, r, j, dom, nnz):
    q = slots[r, j]
    k = q ^ info[0]
    own = (dom - 1) + info[3 + info[0]]
    return jnp.where(q >= dom, q - 1, jnp.where(k == 0, own, k - 1))


def hop_rows(info, slots, lhs, pool, r, dom):
    nnz = lhs.shape[2] // lhs.shape[1]
    rhs = jnp.concatenate([pool[pool_index(info, slots, r, j, dom, nnz)] for j in range(nnz)], 0)
    return jnp.dot(lhs[r], rhs, preferred_element_type=F32)


def hop1_kernel(dom, samples, info, slots, lhs, own, *refs):
    msgs, (cur, total), outs, pool = refs[: dom - 1], refs[dom - 1 : dom + 1], refs[dom + 1 : -1], refs[-1]
    tiles, tile, lanes = own.shape
    feat = lanes // samples
    for i, k in enumerate(partners_1(dom)):

        def put(s, x):
            pool[k - 1, :, s * feat : (s + 1) * feat] = x

        masked_tile(msgs[i][:tile, :], msgs[i][tile : tile + samples, :], put)
    for t in range(tiles):
        pool[dom - 1 + t] = own[t]
    for r in range(tiles):
        hop = hop_rows(info, slots, lhs, pool, r, dom)
        cur[r] = hop.astype(BF16)
        total[r] = hop + own[r].astype(F32)
    for i, k in enumerate(partners(dom)):
        outs[i][...] = cur[info[3 + (info[0] ^ k)]]


def fold(x):
    return functools.reduce(lambda a, b: a + b, [x[i : i + 8] for i in range(0, x.shape[0], 8)])


def prepare_kernel(
    w_in, b_in, w_out_t, b_out, labels, labeled, block, half_w, half_b, wide_w, half_w_t, wide_b, code, same_block
):
    same_block[...] = block[...]
    classes, hidden = w_out_t.shape
    wide = wide_w.shape[1]
    half_w[...] = w_in[...] * jnp.asarray(0.5, BF16)
    half_b[...] = b_in[...] * 0.5
    padded = jnp.concatenate([w_out_t[...], jnp.zeros((wide - classes, hidden), BF16)], 0)
    half_w_t[...] = padded * jnp.asarray(0.5, BF16)
    wide_w[...] = padded.T
    wide_b[...] = jnp.concatenate([b_out[...], jnp.full((1, wide - classes), -1e30, F32)], 1)
    tiles, tile = labels.shape
    rows = jnp.where(labeled[...] != 0, labels[...], -1).astype(F32)
    rows = jnp.concatenate([rows, jnp.zeros((-tiles % 8, tile), F32)], 0)
    code[...] = rows.T.astype(I32)


def mlp_kernel(dom, samples, scale, info, slots, lhs, cur, total, code, half_w, half_b, w_out, half_w_t, b_out, *refs):
    recv = refs[: dom - 1]
    send, x_t, act, dl_t, dpre, bias_acc, cls_acc, pool, slope, prob, dl = refs[dom - 1 :]
    tiles, tile, lanes = cur.shape
    feat = lanes // samples
    hidden = half_w.shape[1]
    wide = w_out.shape[1]
    rows = samples * tile
    nch = hidden // CHUNK
    for i, k in enumerate(partners(dom)):
        pool[k - 1] = recv[i][...]
    for t in range(tiles):
        pool[dom - 1 + t] = cur[t]
    bias_acc[...] = jnp.zeros(bias_acc.shape, F32)
    cls_acc[...] = jnp.zeros(cls_acc.shape, F32)

    def forward(r):
        hop = hop_rows(info, slots, lhs, pool, r, dom)
        xbar = ((total[r] + hop) * XBAR_SCALE).astype(BF16)
        base = r * rows
        for s in range(samples):
            x_t[:, base + s * tile : base + (s + 1) * tile] = xbar[:, s * feat : (s + 1) * feat].T
        batch = BATCH if samples % BATCH == 0 else 1
        for s in range(0, samples, batch):
            x = jnp.concatenate([xbar[:, i * feat : (i + 1) * feat] for i in range(s, s + batch)], 0)
            here = slice(base + s * tile, base + (s + batch) * tile)
            for n in range(nch):
                cols = slice(n * CHUNK, (n + 1) * CHUNK)
                h = jnp.dot(x, half_w[:, cols], preferred_element_type=F32) + half_b[:, cols]
                t = jnp.tanh(h)
                up = 1.0 + t
                silu = h * up
                act[here, cols] = silu.astype(BF16)
                slope[here, cols] = up + silu * (1.0 - t)
            logits = jnp.dot(act[here, :], w_out[...], preferred_element_type=F32) + b_out[...]
            e = jnp.exp(logits)
            prob[here, :] = e * (1.0 / jnp.sum(e, -1, keepdims=True))

    def backward(r):
        base = r * rows
        step = 32
        for c in range(0, tile, step):
            at = [slice(base + s * tile + c, base + s * tile + c + step) for s in range(samples)]
            probs = [prob[one, :] for one in at]
            avg = sum(probs[1:], probs[0]) * (1.0 / samples)
            sq = avg * avg
            sharp = sq * (1.0 / jnp.sum(sq, -1, keepdims=True))
            label = code[c : c + step, r : r + 1]
            hit = jnp.where(lax.broadcasted_iota(I32, (step, wide), 1) == label, scale, 0.0)
            used = jnp.where(label >= 0, scale, 0.0)
            part = jnp.zeros((step, wide), F32)
            for one, p in zip(at, probs):
                off = p - sharp
                inner = jnp.sum(off * p, -1, keepdims=True)
                d = p * ((2.0 * scale) * (off - inner) + used) - hit
                part = part + d
                dl[one, :] = d.astype(BF16)
            cls_acc[...] += fold(part)
        for s in range(samples):
            here = slice(base + s * tile, base + (s + 1) * tile)
            d = dl[here, :]
            dl_t[:, here] = d.T[: dl_t.shape[0]]
            for n in range(nch):
                cols = slice(n * CHUNK, (n + 1) * CHUNK)
                dp = jnp.dot(d, half_w_t[:, cols], preferred_element_type=F32) * slope[here, cols]
                dpre[here, cols] = dp.astype(BF16)
                bias_acc[:, cols] += fold(dp)

    for r in range(tiles + AHEAD):
        if r < tiles:
            forward(r)
        if r >= AHEAD:
            backward(r - AHEAD)
    half_pieces(1 - info[2], x_t, act, dl_t, dpre, bias_acc, cls_acc, lambda m: info[1] ^ m, send)


def half_pieces(core, x_t, act, dl_t, dpre, bias_acc, cls_acc, place, out):
    feat, wide_t = x_t.shape[0], dl_t.shape[0]
    half = act.shape[1] // 2
    wide = cls_acc.shape[1]
    lanes = out.shape[2]
    start = pl.multiple_of(core * half, half)
    chunk = min(CHUNK, half)
    each = chunk // lanes
    cls = jnp.sum(cls_acc[...], 0, keepdims=True)
    first = place(0)
    for n in range(half // chunk):
        cols = pl.ds(start + n * chunk, chunk)
        g_in = jnp.dot(x_t[...], dpre[:, cols], preferred_element_type=F32)
        g_out = jnp.dot(dl_t[...], act[:, cols], preferred_element_type=F32)
        g_bias = jnp.sum(bias_acc[:, cols], 0, keepdims=True)
        for i in range(each):
            at = (n * each + i) ^ first
            part = slice(i * lanes, (i + 1) * lanes)
            out[at, :feat, :] = g_in[:, part]
            out[at, feat : feat + wide_t, :] = g_out[:, part]
            out[at, feat + wide_t :, :] = jnp.concatenate(
                [g_bias[:, part]]
                + [cls[:, j * lanes : (j + 1) * lanes] for j in range(wide // lanes)]
                + [jnp.zeros((TAIL - 1 - wide // lanes, lanes), F32)],
                0,
            )


def keep_kernel(info, x_t, act, dl_t, dpre, bias_acc, cls_acc, keep):
    half_pieces(info[2], x_t, act, dl_t, dpre, bias_acc, cls_acc, lambda m: info[1] ^ m, keep)


def encode(x, feat, n_tail):
    body = x.shape[0] - TAIL
    parts = [x[:feat], x[feat:body]] + [x[body + i : body + i + 1] for i in range(n_tail)]
    ints, exps = [], []
    for p in parts:
        top = jnp.max(jnp.abs(p), 0, keepdims=True)
        e = jnp.floor(jnp.log2(jnp.maximum(top, 1e-30)))
        q = jnp.round(p * jnp.exp2(14.0 - e))
        ints.append(jnp.clip(q, -32767.0, 32767.0).astype(I32))
        exps.append(e.astype(I32))
    used = 2 * n_tail + 2
    last = ints[2:] + exps + [jnp.zeros((2 * TAIL - used, x.shape[1]), I32)]
    return jnp.concatenate(ints[:2] + [jnp.concatenate(last, 0)], 0).astype(I16)


def decode(ref, feat, n_tail):
    body = ref.shape[0] - 2 * TAIL
    v = ref[...].astype(I32).astype(F32)
    last = v[body:]
    scales = jnp.exp2(last[n_tail : 2 * n_tail + 2] - 14.0)
    tail = jnp.concatenate(
        [last[:n_tail] * scales[2:], jnp.zeros((TAIL - n_tail, v.shape[1]), F32)], 0
    )
    return jnp.concatenate([v[:feat] * scales[0:1], v[feat:body] * scales[1:2], tail], 0)


def pair_kernel(feat, n_tail, keep, recv, own, *msgs):
    own[...] = keep[0] + recv[0]
    for m in range(1, keep.shape[0]):
        msgs[m - 1][...] = encode(keep[m] + recv[m], feat, n_tail)


def scatter_kernel(feat, n_tail, n_out, own, *refs):
    total = own[...]
    msgs, outs = refs[: -n_out], refs[-n_out:]
    for ref in msgs:
        total = total + decode(ref, feat, n_tail)
    q = encode(total, feat, n_tail)
    for ref in outs:
        ref[...] = q


def tree_kernel(feat, n_tail, order, *refs):
    n_in = len(order) + 1
    parts = [decode(refs[i], feat, n_tail) for i in [n_in - 1] + [order.index(m) for m in range(len(order))]]
    while len(parts) > 1:
        parts = [a + b for a, b in zip(parts[::2], parts[1::2])]
    q = encode(parts[0], feat, n_tail)
    for ref in refs[n_in:]:
        ref[...] = q


def unpack_kernel(feat, n_tail, classes, info, *refs):
    pieces, (g_in, b_in, g_out, b_out) = refs[:-4], refs[-4:]
    lanes = pieces[0].shape[1]
    half = len(pieces) // 2
    body = pieces[0].shape[0] - 2 * TAIL
    for c in range(2):
        for i, m in enumerate((0,) + (3, 1, 2)):
            at = (info[2] ^ c) * half + (info[1] ^ m)
            x = decode(pieces[c * half + i], feat, n_tail)
            where = pl.ds(pl.multiple_of(at * lanes, lanes), lanes)
            g_in[:, where] = x[:feat]
            g_out[:, where] = x[feat : feat + classes]
            b_in[:, where] = x[body : body + 1]

            @pl.when(at == 0)
            def _():
                for j in range(n_tail - 1):
                    b_out[:, j * lanes : (j + 1) * lanes] = x[body + 1 + j : body + 2 + j]


def xor_permute(x, axis, mask):
    return lax.ppermute(x, axis, [(i, i ^ mask) for i in range(lax.axis_size(axis))])


def swap_all(blocks):
    return [xor_permute(x, "dom", k) for k, x in zip(partners(len(blocks) + 1), blocks)]


def bit_groups(axis, first):
    size, bit, groups = lax.axis_size(axis), first, []
    while (1 << bit) < size:
        groups.append([m << bit for m in (1, 2, 3) if (m << bit) < size])
        bit += 2
    return groups


def reduce_grads(keep, recv, info, feat, n_tail, classes, hidden):
    count, rows, lanes = keep.shape
    coded = like((rows + TAIL, lanes), I16)
    own, *msgs = call(
        functools.partial(pair_kernel, feat, n_tail),
        [like((rows, lanes), F32)] + [coded] * (count - 1),
        [keep, recv],
    )
    msgs = [xor_permute(x, "dp", m + 1) for m, x in enumerate(msgs)]
    groups = [("dom", masks) for masks in bit_groups("dom", 1)] + [("dp", masks) for masks in bit_groups("dp", 2)]
    qs = call(functools.partial(scatter_kernel, feat, n_tail, 4), [coded] * 4, [own] + msgs)
    for axis, masks in groups:
        order = [m for m in (1, 0, 2) if m < len(masks)]
        got = [xor_permute(qs[i + 1], axis, masks[m]) for i, m in enumerate(order)]
        qs = call(functools.partial(tree_kernel, feat, n_tail, order), [coded] * 4, got + [qs[0]])
    pieces = [qs[0]] + [xor_permute(qs[i + 1], "dp", m) for i, m in enumerate((3, 1, 2))]
    pieces = pieces + [xor_permute(x, "dom", 1) for x in pieces]
    return call(
        functools.partial(unpack_kernel, feat, n_tail, classes),
        [like((feat, hidden), F32), like((1, hidden), F32), like((classes, hidden), F32), like((1, (n_tail - 1) * lanes), F32)],
        [info] + pieces,
        n_smem=1,
    )


def per_device(
    features,
    keep_masks,
    serve_ids,
    col_slot,
    adj_blocks,
    node_labels,
    labeled,
    weight_in,
    bias_in,
    weight_out,
    bias_out,
):
    tiles, nnz = col_slot.shape[1:]
    tile = adj_blocks.shape[-1]
    feat = features.shape[-1]
    samples = keep_masks.shape[1]
    hidden, classes = weight_out.shape
    dom = lax.axis_size("dom")
    me = lax.axis_index("dom")
    place = jnp.stack([me, lax.axis_index("dp") & 3, me & 1]).astype(I32)
    info = jnp.concatenate([place, serve_ids.reshape(-1)])
    adj = adj_blocks[0]
    feats = features.reshape(tiles, tile, feat)
    masks = keep_masks[0]
    lanes = samples * feat
    wide = -(-classes // 128) * 128

    rows = jnp.pad(masks.reshape(samples, tiles, tile).transpose(1, 0, 2), ((0, 0), (0, 16 - samples), (0, 0)))
    both = jnp.concatenate([feats, rows], 1)
    *msgs, both = call(
        select_kernel, [like((tile + 16, feat), BF16)] * (dom - 1) + [like(both.shape, BF16)], [info, both], n_smem=1
    )
    lhs, own, slots = call(
        functools.partial(layout_kernel, samples),
        [like((tiles, tile, nnz * tile), BF16), like((tiles, tile, lanes), BF16), like((tiles, nnz), I32)],
        [both, adj, col_slot[0]],
    )
    msgs = [xor_permute(x, "dom", k) for k, x in zip(partners_1(dom), msgs)]
    cur, total, *outs = call(
        functools.partial(hop1_kernel, dom, samples),
        [like((tiles, tile, lanes), BF16), like((tiles, tile, lanes), F32)] + [like((tile, lanes), BF16)] * (dom - 1),
        [info, slots, lhs, own] + msgs,
        [pltpu.VMEM((dom - 1 + tiles, tile, lanes), BF16)],
        n_smem=2,
    )
    late = min(LATE, dom - 2)
    half_w, half_b, w_out, half_w_t, b_out, code, outs[late] = call(
        prepare_kernel,
        [
            like((feat, hidden), BF16),
            like((1, hidden), F32),
            like((hidden, wide), BF16),
            like((wide, hidden), BF16),
            like((1, wide), F32),
            like((tile, -(-tiles // 8) * 8), I32),
            like(outs[late].shape, BF16),
        ],
        [weight_in, bias_in.reshape(1, hidden), weight_out.T, bias_out.reshape(1, classes)]
        + [node_labels.reshape(tiles, tile), labeled.reshape(tiles, tile), outs[late]],
    )
    outs = swap_all(outs)
    rows = samples * tile * tiles
    wide_t = -(-classes // 16) * 16
    half = like((hidden // 256, feat + wide_t + TAIL, 128), F32)
    send, *held = call(
        functools.partial(mlp_kernel, dom, samples, 1.0 / (samples * tiles * tile)),
        [
            half,
            like((feat, rows), BF16),
            like((rows, hidden), BF16),
            like((wide_t, rows), BF16),
            like((rows, hidden), BF16),
            like((8, hidden), F32),
            like((8, wide), F32),
        ],
        [info, slots, lhs, cur, total, code, half_w, half_b, w_out, half_w_t, b_out] + outs,
        [
            pltpu.VMEM((dom - 1 + tiles, tile, lanes), BF16),
            pltpu.VMEM((rows, hidden), F32),
            pltpu.VMEM((rows, wide), F32),
            pltpu.VMEM((rows, wide), BF16),
        ],
        n_smem=2,
        vmem=24,
    )
    recv = xor_permute(send, "dom", 1)
    keep = call(keep_kernel, half, [info] + held, n_smem=1)
    g_in, b_in, g_out, b_out = reduce_grads(keep, recv, info, feat, 1 + wide // 128, classes, hidden)
    return g_in, b_in.reshape(hidden), g_out.T, b_out.reshape(-1)[:classes]


def solution(mesh):
    placed = (
        P("dp", "dom", None),
        P("dp", None, "dom"),
        P("dp", "dom", None, None),
        P("dp", "dom", None),
        P("dp", "dom", None, None, None),
        P("dp", "dom"),
        P("dp", "dom"),
        P(),
        P(),
        P(),
        P(),
    )
    return jax.shard_map(
        per_device, mesh=mesh, in_specs=placed, out_specs=(P(), P(), P(), P()), check_vma=False
    )
```

```python
import functools

import jax
import jax.numpy as jnp
from jax import lax
from jax.experimental import pallas as pl
from jax.experimental.pallas import tpu as pltpu
from jax.sharding import PartitionSpec as P

ORDER = 2
KEEP_RATE = 0.5
XBAR_SCALE = 1.0 / ((ORDER + 1) * KEEP_RATE)
F32, BF16, I16, I32 = jnp.float32, jnp.bfloat16, jnp.int16, jnp.int32
MIB = 1024 * 1024
SMEM = pl.BlockSpec(memory_space=pltpu.SMEM)
VMEM = pl.BlockSpec(memory_space=pltpu.VMEM)
CHUNK = 256
AHEAD = 2
BATCH = 4
LATE = 4
TAIL = 8


def call(kernel, outs, ins, scratch=(), n_smem=0, vmem=8):
    return pl.pallas_call(
        kernel,
        out_shape=outs,
        in_specs=[SMEM] * n_smem + [VMEM] * (len(ins) - n_smem),
        out_specs=jax.tree.map(lambda _: VMEM, outs),
        scratch_shapes=list(scratch),
        compiler_params=pltpu.CompilerParams(vmem_limit_bytes=vmem * MIB),
    )(*ins)


def like(shape, dtype):
    return jax.ShapeDtypeStruct(shape, dtype)


def tops(dom):
    return [1 << b for b in reversed(range((dom - 1).bit_length()))]


def partners(dom):
    return [k for odd in (0, 1) for top in tops(dom) for k in range(top, 2 * top) if k % 2 == odd]


def partners_1(dom):
    return [k for top in tops(dom) for odd in (0, 1) for k in range(top, 2 * top) if k % 2 == odd]


def select_kernel(info, tiles, *refs):
    msgs = refs[:-1]
    refs[-1][...] = tiles[...]
    for i, k in enumerate(partners_1(len(msgs) + 1)):
        msgs[i][...] = tiles[info[3 + (info[0] ^ k)]]


def masked_tile(f, m, put):
    samples, tile = m.shape
    cols = jnp.concatenate([m.astype(F32), jnp.zeros((8 - samples, tile), F32)], 0).T
    f = f.astype(F32)
    for s in range(samples):
        put(s, (f * cols[:, s : s + 1]).astype(BF16))


def layout_kernel(samples, both, adj, slots, lhs, own, same_slots):
    same_slots[...] = slots[...]
    tiles, tile, lanes = own.shape
    feat = lanes // samples
    for t in range(tiles):
        lhs[t] = jnp.concatenate([adj[t, j] for j in range(adj.shape[1])], 1)

        def put(s, x):
            own[t, :, s * feat : (s + 1) * feat] = x

        masked_tile(both[t, :tile, :], both[t, tile : tile + samples, :], put)


def pool_index(info, slots, r, j, dom, nnz):
    q = slots[r, j]
    k = q ^ info[0]
    own = (dom - 1) + info[3 + info[0]]
    return jnp.where(q >= dom, q - 1, jnp.where(k == 0, own, k - 1))


def hop_rows(info, slots, lhs, pool, r, dom):
    nnz = lhs.shape[2] // lhs.shape[1]
    rhs = jnp.concatenate([pool[pool_index(info, slots, r, j, dom, nnz)] for j in range(nnz)], 0)
    return jnp.dot(lhs[r], rhs, preferred_element_type=F32)


def hop1_kernel(dom, samples, info, slots, lhs, own, *refs):
    msgs, (cur, total), outs, pool = refs[: dom - 1], refs[dom - 1 : dom + 1], refs[dom + 1 : -1], refs[-1]
    tiles, tile, lanes = own.shape
    feat = lanes // samples
    for i, k in enumerate(partners_1(dom)):

        def put(s, x):
            pool[k - 1, :, s * feat : (s + 1) * feat] = x

        masked_tile(msgs[i][:tile, :], msgs[i][tile : tile + samples, :], put)
    for t in range(tiles):
        pool[dom - 1 + t] = own[t]
    for r in range(tiles):
        hop = hop_rows(info, slots, lhs, pool, r, dom)
        cur[r] = hop.astype(BF16)
        total[r] = hop + own[r].astype(F32)
    for i, k in enumerate(partners(dom)):
        outs[i][...] = cur[info[3 + (info[0] ^ k)]]


def fold(x):
    return functools.reduce(lambda a, b: a + b, [x[i : i + 8] for i in range(0, x.shape[0], 8)])


def prepare_kernel(
    w_in, b_in, w_out_t, b_out, labels, labeled, block, half_w, half_b, wide_w, half_w_t, wide_b, code, same_block
):
    same_block[...] = block[...]
    classes, hidden = w_out_t.shape
    wide = wide_w.shape[1]
    half_w[...] = w_in[...] * jnp.asarray(0.5, BF16)
    half_b[...] = b_in[...] * 0.5
    padded = jnp.concatenate([w_out_t[...], jnp.zeros((wide - classes, hidden), BF16)], 0)
    half_w_t[...] = padded * jnp.asarray(0.5, BF16)
    wide_w[...] = padded.T
    wide_b[...] = jnp.concatenate([b_out[...], jnp.full((1, wide - classes), -1e30, F32)], 1)
    tiles, tile = labels.shape
    rows = jnp.where(labeled[...] != 0, labels[...], -1).astype(F32)
    rows = jnp.concatenate([rows, jnp.zeros((-tiles % 8, tile), F32)], 0)
    code[...] = rows.T.astype(I32)


def mlp_kernel(dom, samples, scale, info, slots, lhs, cur, total, code, half_w, half_b, w_out, half_w_t, b_out, *refs):
    recv = refs[: dom - 1]
    send, x_t, act, dl_t, dpre, bias_acc, cls_acc, pool, slope, prob, dl = refs[dom - 1 :]
    tiles, tile, lanes = cur.shape
    feat = lanes // samples
    hidden = half_w.shape[1]
    wide = w_out.shape[1]
    rows = samples * tile
    nch = hidden // CHUNK
    for i, k in enumerate(partners(dom)):
        pool[k - 1] = recv[i][...]
    for t in range(tiles):
        pool[dom - 1 + t] = cur[t]
    bias_acc[...] = jnp.zeros(bias_acc.shape, F32)
    cls_acc[...] = jnp.zeros(cls_acc.shape, F32)

    def forward(r):
        hop = hop_rows(info, slots, lhs, pool, r, dom)
        xbar = ((total[r] + hop) * XBAR_SCALE).astype(BF16)
        base = r * rows
        for s in range(samples):
            x_t[:, base + s * tile : base + (s + 1) * tile] = xbar[:, s * feat : (s + 1) * feat].T
        batch = BATCH if samples % BATCH == 0 else 1
        for s in range(0, samples, batch):
            x = jnp.concatenate([xbar[:, i * feat : (i + 1) * feat] for i in range(s, s + batch)], 0)
            here = slice(base + s * tile, base + (s + batch) * tile)
            for n in range(nch):
                cols = slice(n * CHUNK, (n + 1) * CHUNK)
                h = jnp.dot(x, half_w[:, cols], preferred_element_type=F32) + half_b[:, cols]
                t = jnp.tanh(h)
                up = 1.0 + t
                silu = h * up
                act[here, cols] = silu.astype(BF16)
                slope[here, cols] = up + silu * (1.0 - t)
            logits = jnp.dot(act[here, :], w_out[...], preferred_element_type=F32) + b_out[...]
            e = jnp.exp(logits)
            norm = jnp.sum(e, -1, keepdims=True)
            shrink = jnp.where(norm > 2.0**64, 2.0**-64, 1.0)
            prob[here, :] = (e * shrink) * (1.0 / (norm * shrink))

    def backward(r):
        base = r * rows
        step = 32
        for c in range(0, tile, step):
            at = [slice(base + s * tile + c, base + s * tile + c + step) for s in range(samples)]
            probs = [prob[one, :] for one in at]
            avg = sum(probs[1:], probs[0]) * (1.0 / samples)
            sq = avg * avg
            sharp = sq * (1.0 / jnp.sum(sq, -1, keepdims=True))
            label = code[c : c + step, r : r + 1]
            hit = jnp.where(lax.broadcasted_iota(I32, (step, wide), 1) == label, scale, 0.0)
            used = jnp.where(label >= 0, scale, 0.0)
            part = jnp.zeros((step, wide), F32)
            for one, p in zip(at, probs):
                off = p - sharp
                inner = jnp.sum(off * p, -1, keepdims=True)
                d = p * ((2.0 * scale) * (off - inner) + used) - hit
                part = part + d
                dl[one, :] = d.astype(BF16)
            cls_acc[...] += fold(part)
        for s in range(samples):
            here = slice(base + s * tile, base + (s + 1) * tile)
            d = dl[here, :]
            dl_t[:, here] = d.T[: dl_t.shape[0]]
            for n in range(nch):
                cols = slice(n * CHUNK, (n + 1) * CHUNK)
                dp = jnp.dot(d, half_w_t[:, cols], preferred_element_type=F32) * slope[here, cols]
                dpre[here, cols] = dp.astype(BF16)
                bias_acc[:, cols] += fold(dp)

    for r in range(tiles + AHEAD):
        if r < tiles:
            forward(r)
        if r >= AHEAD:
            backward(r - AHEAD)
    half_pieces(1 - info[2], x_t, act, dl_t, dpre, bias_acc, cls_acc, lambda m: info[1] ^ m, send)


def half_pieces(core, x_t, act, dl_t, dpre, bias_acc, cls_acc, place, out):
    feat, wide_t = x_t.shape[0], dl_t.shape[0]
    half = act.shape[1] // 2
    wide = cls_acc.shape[1]
    lanes = out.shape[2]
    start = pl.multiple_of(core * half, half)
    chunk = min(CHUNK, half)
    each = chunk // lanes
    cls = jnp.sum(cls_acc[...], 0, keepdims=True)
    first = place(0)
    for n in range(half // chunk):
        cols = pl.ds(start + n * chunk, chunk)
        g_in = jnp.dot(x_t[...], dpre[:, cols], preferred_element_type=F32)
        g_out = jnp.dot(dl_t[...], act[:, cols], preferred_element_type=F32)
        g_bias = jnp.sum(bias_acc[:, cols], 0, keepdims=True)
        for i in range(each):
            at = (n * each + i) ^ first
            part = slice(i * lanes, (i + 1) * lanes)
            out[at, :feat, :] = g_in[:, part]
            out[at, feat : feat + wide_t, :] = g_out[:, part]
            out[at, feat + wide_t :, :] = jnp.concatenate(
                [g_bias[:, part]]
                + [cls[:, j * lanes : (j + 1) * lanes] for j in range(wide // lanes)]
                + [jnp.zeros((TAIL - 1 - wide // lanes, lanes), F32)],
                0,
            )


def keep_kernel(info, x_t, act, dl_t, dpre, bias_acc, cls_acc, keep):
    half_pieces(info[2], x_t, act, dl_t, dpre, bias_acc, cls_acc, lambda m: info[1] ^ m, keep)


def encode(x, feat, n_tail):
    body = x.shape[0] - TAIL
    parts = [x[:feat], x[feat:body]] + [x[body + i : body + i + 1] for i in range(n_tail)]
    ints, exps = [], []
    for p in parts:
        top = jnp.max(jnp.abs(p), 0, keepdims=True)
        e = jnp.floor(jnp.log2(jnp.maximum(top, 1e-30)))
        q = jnp.round(p * jnp.exp2(14.0 - e))
        ints.append(jnp.clip(q, -32767.0, 32767.0).astype(I32))
        exps.append(e.astype(I32))
    used = 2 * n_tail + 2
    last = ints[2:] + exps + [jnp.zeros((2 * TAIL - used, x.shape[1]), I32)]
    return jnp.concatenate(ints[:2] + [jnp.concatenate(last, 0)], 0).astype(I16)


def decode(ref, feat, n_tail):
    body = ref.shape[0] - 2 * TAIL
    v = ref[...].astype(I32).astype(F32)
    last = v[body:]
    scales = jnp.exp2(last[n_tail : 2 * n_tail + 2] - 14.0)
    tail = jnp.concatenate(
        [last[:n_tail] * scales[2:], jnp.zeros((TAIL - n_tail, v.shape[1]), F32)], 0
    )
    return jnp.concatenate([v[:feat] * scales[0:1], v[feat:body] * scales[1:2], tail], 0)


def pair_kernel(feat, n_tail, keep, recv, own, *msgs):
    own[...] = keep[0] + recv[0]
    for m in range(1, keep.shape[0]):
        msgs[m - 1][...] = encode(keep[m] + recv[m], feat, n_tail)


def scatter_kernel(feat, n_tail, n_out, own, *refs):
    total = own[...]
    msgs, outs = refs[: -n_out], refs[-n_out:]
    for ref in msgs:
        total = total + decode(ref, feat, n_tail)
    q = encode(total, feat, n_tail)
    for ref in outs:
        ref[...] = q


def tree_kernel(feat, n_tail, order, *refs):
    n_in = len(order) + 1
    parts = [decode(refs[i], feat, n_tail) for i in [n_in - 1] + [order.index(m) for m in range(len(order))]]
    while len(parts) > 1:
        parts = [a + b for a, b in zip(parts[::2], parts[1::2])]
    q = encode(parts[0], feat, n_tail)
    for ref in refs[n_in:]:
        ref[...] = q


def unpack_kernel(feat, n_tail, classes, info, *refs):
    pieces, (g_in, b_in, g_out, b_out) = refs[:-4], refs[-4:]
    lanes = pieces[0].shape[1]
    half = len(pieces) // 2
    body = pieces[0].shape[0] - 2 * TAIL
    for c in range(2):
        for i, m in enumerate((0,) + (3, 1, 2)):
            at = (info[2] ^ c) * half + (info[1] ^ m)
            x = decode(pieces[c * half + i], feat, n_tail)
            where = pl.ds(pl.multiple_of(at * lanes, lanes), lanes)
            g_in[:, where] = x[:feat]
            g_out[:, where] = x[feat : feat + classes]
            b_in[:, where] = x[body : body + 1]

            @pl.when(at == 0)
            def _():
                for j in range(n_tail - 1):
                    b_out[:, j * lanes : (j + 1) * lanes] = x[body + 1 + j : body + 2 + j]


def xor_permute(x, axis, mask):
    return lax.ppermute(x, axis, [(i, i ^ mask) for i in range(lax.axis_size(axis))])


def swap_all(blocks):
    return [xor_permute(x, "dom", k) for k, x in zip(partners(len(blocks) + 1), blocks)]


def bit_groups(axis, first):
    size, bit, groups = lax.axis_size(axis), first, []
    while (1 << bit) < size:
        groups.append([m << bit for m in (1, 2, 3) if (m << bit) < size])
        bit += 2
    return groups


def reduce_grads(keep, recv, info, feat, n_tail, classes, hidden):
    count, rows, lanes = keep.shape
    coded = like((rows + TAIL, lanes), I16)
    own, *msgs = call(
        functools.partial(pair_kernel, feat, n_tail),
        [like((rows, lanes), F32)] + [coded] * (count - 1),
        [keep, recv],
    )
    msgs = [xor_permute(x, "dp", m + 1) for m, x in enumerate(msgs)]
    groups = [("dom", masks) for masks in bit_groups("dom", 1)] + [("dp", masks) for masks in bit_groups("dp", 2)]
    qs = call(functools.partial(scatter_kernel, feat, n_tail, 4), [coded] * 4, [own] + msgs)
    for axis, masks in groups:
        order = [m for m in (1, 0, 2) if m < len(masks)]
        got = [xor_permute(qs[i + 1], axis, masks[m]) for i, m in enumerate(order)]
        qs = call(functools.partial(tree_kernel, feat, n_tail, order), [coded] * 4, got + [qs[0]])
    pieces = [qs[0]] + [xor_permute(qs[i + 1], "dp", m) for i, m in enumerate((3, 1, 2))]
    pieces = pieces + [xor_permute(x, "dom", 1) for x in pieces]
    return call(
        functools.partial(unpack_kernel, feat, n_tail, classes),
        [like((feat, hidden), F32), like((1, hidden), F32), like((classes, hidden), F32), like((1, (n_tail - 1) * lanes), F32)],
        [info] + pieces,
        n_smem=1,
    )


def per_device(
    features,
    keep_masks,
    serve_ids,
    col_slot,
    adj_blocks,
    node_labels,
    labeled,
    weight_in,
    bias_in,
    weight_out,
    bias_out,
):
    tiles, nnz = col_slot.shape[1:]
    tile = adj_blocks.shape[-1]
    feat = features.shape[-1]
    samples = keep_masks.shape[1]
    hidden, classes = weight_out.shape
    dom = lax.axis_size("dom")
    me = lax.axis_index("dom")
    place = jnp.stack([me, lax.axis_index("dp") & 3, me & 1]).astype(I32)
    info = jnp.concatenate([place, serve_ids.reshape(-1)])
    adj = adj_blocks[0]
    feats = features.reshape(tiles, tile, feat)
    masks = keep_masks[0]
    lanes = samples * feat
    wide = -(-classes // 128) * 128

    rows = jnp.pad(masks.reshape(samples, tiles, tile).transpose(1, 0, 2), ((0, 0), (0, 16 - samples), (0, 0)))
    both = jnp.concatenate([feats, rows], 1)
    *msgs, both = call(
        select_kernel, [like((tile + 16, feat), BF16)] * (dom - 1) + [like(both.shape, BF16)], [info, both], n_smem=1
    )
    lhs, own, slots = call(
        functools.partial(layout_kernel, samples),
        [like((tiles, tile, nnz * tile), BF16), like((tiles, tile, lanes), BF16), like((tiles, nnz), I32)],
        [both, adj, col_slot[0]],
    )
    msgs = [xor_permute(x, "dom", k) for k, x in zip(partners_1(dom), msgs)]
    cur, total, *outs = call(
        functools.partial(hop1_kernel, dom, samples),
        [like((tiles, tile, lanes), BF16), like((tiles, tile, lanes), F32)] + [like((tile, lanes), BF16)] * (dom - 1),
        [info, slots, lhs, own] + msgs,
        [pltpu.VMEM((dom - 1 + tiles, tile, lanes), BF16)],
        n_smem=2,
    )
    late = min(LATE, dom - 2)
    half_w, half_b, w_out, half_w_t, b_out, code, outs[late] = call(
        prepare_kernel,
        [
            like((feat, hidden), BF16),
            like((1, hidden), F32),
            like((hidden, wide), BF16),
            like((wide, hidden), BF16),
            like((1, wide), F32),
            like((tile, -(-tiles // 8) * 8), I32),
            like(outs[late].shape, BF16),
        ],
        [weight_in, bias_in.reshape(1, hidden), weight_out.T, bias_out.reshape(1, classes)]
        + [node_labels.reshape(tiles, tile), labeled.reshape(tiles, tile), outs[late]],
    )
    outs = swap_all(outs)
    rows = samples * tile * tiles
    wide_t = -(-classes // 16) * 16
    half = like((hidden // 256, feat + wide_t + TAIL, 128), F32)
    send, *held = call(
        functools.partial(mlp_kernel, dom, samples, 1.0 / (samples * tiles * tile)),
        [
            half,
            like((feat, rows), BF16),
            like((rows, hidden), BF16),
            like((wide_t, rows), BF16),
            like((rows, hidden), BF16),
            like((8, hidden), F32),
            like((8, wide), F32),
        ],
        [info, slots, lhs, cur, total, code, half_w, half_b, w_out, half_w_t, b_out] + outs,
        [
            pltpu.VMEM((dom - 1 + tiles, tile, lanes), BF16),
            pltpu.VMEM((rows, hidden), F32),
            pltpu.VMEM((rows, wide), F32),
            pltpu.VMEM((rows, wide), BF16),
        ],
        n_smem=2,
        vmem=24,
    )
    recv = xor_permute(send, "dom", 1)
    keep = call(keep_kernel, half, [info] + held, n_smem=1)
    g_in, b_in, g_out, b_out = reduce_grads(keep, recv, info, feat, 1 + wide // 128, classes, hidden)
    return g_in, b_in.reshape(hidden), g_out.T, b_out.reshape(-1)[:classes]


def solution(mesh):
    placed = (
        P("dp", "dom", None),
        P("dp", None, "dom"),
        P("dp", "dom", None, None),
        P("dp", "dom", None),
        P("dp", "dom", None, None, None),
        P("dp", "dom"),
        P("dp", "dom"),
        P(),
        P(),
        P(),
        P(),
    )
    return jax.shard_map(
        per_device, mesh=mesh, in_specs=placed, out_specs=(P(), P(), P(), P()), check_vma=False
    )
```

```python
import functools

import jax
import jax.numpy as jnp
from jax import lax
from jax.experimental import pallas as pl
from jax.experimental.pallas import tpu as pltpu
from jax.sharding import PartitionSpec as P

ORDER = 2
KEEP_RATE = 0.5
XBAR_SCALE = 1.0 / ((ORDER + 1) * KEEP_RATE)
F32, BF16, I16, I32 = jnp.float32, jnp.bfloat16, jnp.int16, jnp.int32
MIB = 1024 * 1024
SMEM = pl.BlockSpec(memory_space=pltpu.SMEM)
VMEM = pl.BlockSpec(memory_space=pltpu.VMEM)
CHUNK = 256
AHEAD = 2
BATCH = 4
LATE = 4
TAIL = 8


def call(kernel, outs, ins, scratch=(), n_smem=0, vmem=8):
    return pl.pallas_call(
        kernel,
        out_shape=outs,
        in_specs=[SMEM] * n_smem + [VMEM] * (len(ins) - n_smem),
        out_specs=jax.tree.map(lambda _: VMEM, outs),
        scratch_shapes=list(scratch),
        compiler_params=pltpu.CompilerParams(vmem_limit_bytes=vmem * MIB),
    )(*ins)


def like(shape, dtype):
    return jax.ShapeDtypeStruct(shape, dtype)


def tops(dom):
    return [1 << b for b in reversed(range((dom - 1).bit_length()))]


def partners(dom):
    masks = []
    for odd in (0, 1):
        far = [k for k in range(dom // 2, dom) if k % 2 == odd]
        near = [k for k in range(dom // 2 - 1, 0, -1) if k % 2 == odd]
        for i in range(len(far)):
            masks += far[i : i + 1] + near[i : i + 1]
    return masks


def partners_1(dom):
    return [k for top in tops(dom) for odd in (0, 1) for k in range(top, 2 * top) if k % 2 == odd]


def select_kernel(info, tiles, *refs):
    msgs = refs[:-1]
    refs[-1][...] = tiles[...]
    for i, k in enumerate(partners_1(len(msgs) + 1)):
        msgs[i][...] = tiles[info[3 + (info[0] ^ k)]]


def masked_tile(f, m, put):
    samples, tile = m.shape
    cols = jnp.concatenate([m.astype(F32), jnp.zeros((8 - samples, tile), F32)], 0).T
    f = f.astype(F32)
    for s in range(samples):
        put(s, (f * cols[:, s : s + 1]).astype(BF16))


def layout_kernel(samples, both, adj, slots, lhs, own, same_slots):
    same_slots[...] = slots[...]
    tiles, tile, lanes = own.shape
    feat = lanes // samples
    for t in range(tiles):
        lhs[t] = jnp.concatenate([adj[t, j] for j in range(adj.shape[1])], 1)

        def put(s, x):
            own[t, :, s * feat : (s + 1) * feat] = x

        masked_tile(both[t, :tile, :], both[t, tile : tile + samples, :], put)


def pool_index(info, slots, r, j, dom, nnz):
    q = slots[r, j]
    k = q ^ info[0]
    own = (dom - 1) + info[3 + info[0]]
    return jnp.where(q >= dom, q - 1, jnp.where(k == 0, own, k - 1))


def hop_rows(info, slots, lhs, pool, r, dom):
    nnz = lhs.shape[2] // lhs.shape[1]
    rhs = jnp.concatenate([pool[pool_index(info, slots, r, j, dom, nnz)] for j in range(nnz)], 0)
    return jnp.dot(lhs[r], rhs, preferred_element_type=F32)


def hop1_kernel(dom, samples, info, slots, lhs, own, *refs):
    msgs, (cur, total), outs, pool = refs[: dom - 1], refs[dom - 1 : dom + 1], refs[dom + 1 : -1], refs[-1]
    tiles, tile, lanes = own.shape
    feat = lanes // samples
    for i, k in enumerate(partners_1(dom)):

        def put(s, x):
            pool[k - 1, :, s * feat : (s + 1) * feat] = x

        masked_tile(msgs[i][:tile, :], msgs[i][tile : tile + samples, :], put)
    for t in range(tiles):
        pool[dom - 1 + t] = own[t]
    for r in range(tiles):
        hop = hop_rows(info, slots, lhs, pool, r, dom)
        cur[r] = hop.astype(BF16)
        total[r] = hop + own[r].astype(F32)
    for i, k in enumerate(partners(dom)):
        outs[i][...] = cur[info[3 + (info[0] ^ k)]]


def fold(x):
    return functools.reduce(lambda a, b: a + b, [x[i : i + 8] for i in range(0, x.shape[0], 8)])


def prepare_kernel(
    w_in, b_in, w_out_t, b_out, labels, labeled, block, half_w, half_b, wide_w, half_w_t, wide_b, code, same_block
):
    same_block[...] = block[...]
    classes, hidden = w_out_t.shape
    wide = wide_w.shape[1]
    half_w[...] = w_in[...] * jnp.asarray(0.5, BF16)
    half_b[...] = b_in[...] * 0.5
    padded = jnp.concatenate([w_out_t[...], jnp.zeros((wide - classes, hidden), BF16)], 0)
    half_w_t[...] = padded * jnp.asarray(0.5, BF16)
    wide_w[...] = padded.T
    wide_b[...] = jnp.concatenate([b_out[...], jnp.full((1, wide - classes), -1e30, F32)], 1)
    tiles, tile = labels.shape
    rows = jnp.where(labeled[...] != 0, labels[...], -1).astype(F32)
    rows = jnp.concatenate([rows, jnp.zeros((-tiles % 8, tile), F32)], 0)
    code[...] = rows.T.astype(I32)


def mlp_kernel(dom, samples, scale, info, slots, lhs, cur, total, code, half_w, half_b, w_out, half_w_t, b_out, *refs):
    recv = refs[: dom - 1]
    send, x_t, act, dl_t, dpre, bias_acc, cls_acc, pool, slope, prob, dl = refs[dom - 1 :]
    tiles, tile, lanes = cur.shape
    feat = lanes // samples
    hidden = half_w.shape[1]
    wide = w_out.shape[1]
    rows = samples * tile
    nch = hidden // CHUNK
    for i, k in enumerate(partners(dom)):
        pool[k - 1] = recv[i][...]
    for t in range(tiles):
        pool[dom - 1 + t] = cur[t]
    bias_acc[...] = jnp.zeros(bias_acc.shape, F32)
    cls_acc[...] = jnp.zeros(cls_acc.shape, F32)

    def forward(r):
        hop = hop_rows(info, slots, lhs, pool, r, dom)
        xbar = ((total[r] + hop) * XBAR_SCALE).astype(BF16)
        base = r * rows
        for s in range(samples):
            x_t[:, base + s * tile : base + (s + 1) * tile] = xbar[:, s * feat : (s + 1) * feat].T
        batch = BATCH if samples % BATCH == 0 else 1
        for s in range(0, samples, batch):
            x = jnp.concatenate([xbar[:, i * feat : (i + 1) * feat] for i in range(s, s + batch)], 0)
            here = slice(base + s * tile, base + (s + batch) * tile)
            for n in range(nch):
                cols = slice(n * CHUNK, (n + 1) * CHUNK)
                h = jnp.dot(x, half_w[:, cols], preferred_element_type=F32) + half_b[:, cols]
                t = jnp.tanh(h)
                up = 1.0 + t
                silu = h * up
                act[here, cols] = silu.astype(BF16)
                slope[here, cols] = up + silu * (1.0 - t)
            logits = jnp.dot(act[here, :], w_out[...], preferred_element_type=F32) + b_out[...]
            e = jnp.exp(logits)
            norm = jnp.sum(e, -1, keepdims=True)
            shrink = jnp.where(norm > 2.0**64, 2.0**-64, 1.0)
            prob[here, :] = (e * shrink) * (1.0 / (norm * shrink))

    def backward(r):
        base = r * rows
        step = 32
        for c in range(0, tile, step):
            at = [slice(base + s * tile + c, base + s * tile + c + step) for s in range(samples)]
            probs = [prob[one, :] for one in at]
            avg = sum(probs[1:], probs[0]) * (1.0 / samples)
            sq = avg * avg
            sharp = sq * (1.0 / jnp.sum(sq, -1, keepdims=True))
            label = code[c : c + step, r : r + 1]
            hit = jnp.where(lax.broadcasted_iota(I32, (step, wide), 1) == label, scale, 0.0)
            used = jnp.where(label >= 0, scale, 0.0)
            part = jnp.zeros((step, wide), F32)
            for one, p in zip(at, probs):
                off = p - sharp
                inner = jnp.sum(off * p, -1, keepdims=True)
                d = p * ((2.0 * scale) * (off - inner) + used) - hit
                part = part + d
                dl[one, :] = d.astype(BF16)
            cls_acc[...] += fold(part)
        for s in range(samples):
            here = slice(base + s * tile, base + (s + 1) * tile)
            d = dl[here, :]
            dl_t[:, here] = d.T[: dl_t.shape[0]]
            for n in range(nch):
                cols = slice(n * CHUNK, (n + 1) * CHUNK)
                dp = jnp.dot(d, half_w_t[:, cols], preferred_element_type=F32) * slope[here, cols]
                dpre[here, cols] = dp.astype(BF16)
                bias_acc[:, cols] += fold(dp)

    for r in range(tiles + AHEAD):
        if r < tiles:
            forward(r)
        if r >= AHEAD:
            backward(r - AHEAD)
    half_pieces(1 - info[2], x_t, act, dl_t, dpre, bias_acc, cls_acc, lambda m: info[1] ^ m, send)


def half_pieces(core, x_t, act, dl_t, dpre, bias_acc, cls_acc, place, out):
    feat, wide_t = x_t.shape[0], dl_t.shape[0]
    half = act.shape[1] // 2
    wide = cls_acc.shape[1]
    lanes = out.shape[2]
    start = pl.multiple_of(core * half, half)
    chunk = min(CHUNK, half)
    each = chunk // lanes
    cls = jnp.sum(cls_acc[...], 0, keepdims=True)
    first = place(0)
    for n in range(half // chunk):
        cols = pl.ds(start + n * chunk, chunk)
        g_in = jnp.dot(x_t[...], dpre[:, cols], preferred_element_type=F32)
        g_out = jnp.dot(dl_t[...], act[:, cols], preferred_element_type=F32)
        g_bias = jnp.sum(bias_acc[:, cols], 0, keepdims=True)
        for i in range(each):
            at = (n * each + i) ^ first
            part = slice(i * lanes, (i + 1) * lanes)
            out[at, :feat, :] = g_in[:, part]
            out[at, feat : feat + wide_t, :] = g_out[:, part]
            out[at, feat + wide_t :, :] = jnp.concatenate(
                [g_bias[:, part]]
                + [cls[:, j * lanes : (j + 1) * lanes] for j in range(wide // lanes)]
                + [jnp.zeros((TAIL - 1 - wide // lanes, lanes), F32)],
                0,
            )


def keep_kernel(info, x_t, act, dl_t, dpre, bias_acc, cls_acc, keep):
    half_pieces(info[2], x_t, act, dl_t, dpre, bias_acc, cls_acc, lambda m: info[1] ^ m, keep)


def encode(x, feat, n_tail):
    body = x.shape[0] - TAIL
    parts = [x[:feat], x[feat:body]] + [x[body + i : body + i + 1] for i in range(n_tail)]
    ints, exps = [], []
    for p in parts:
        top = jnp.max(jnp.abs(p), 0, keepdims=True)
        e = jnp.floor(jnp.log2(jnp.maximum(top, 1e-30)))
        q = jnp.round(p * jnp.exp2(14.0 - e))
        ints.append(jnp.clip(q, -32767.0, 32767.0).astype(I32))
        exps.append(e.astype(I32))
    used = 2 * n_tail + 2
    last = ints[2:] + exps + [jnp.zeros((2 * TAIL - used, x.shape[1]), I32)]
    return jnp.concatenate(ints[:2] + [jnp.concatenate(last, 0)], 0).astype(I16)


def decode(ref, feat, n_tail):
    body = ref.shape[0] - 2 * TAIL
    v = ref[...].astype(I32).astype(F32)
    last = v[body:]
    scales = jnp.exp2(last[n_tail : 2 * n_tail + 2] - 14.0)
    tail = jnp.concatenate(
        [last[:n_tail] * scales[2:], jnp.zeros((TAIL - n_tail, v.shape[1]), F32)], 0
    )
    return jnp.concatenate([v[:feat] * scales[0:1], v[feat:body] * scales[1:2], tail], 0)


def pair_kernel(feat, n_tail, keep, recv, own, *msgs):
    own[...] = keep[0] + recv[0]
    for m in range(1, keep.shape[0]):
        msgs[m - 1][...] = encode(keep[m] + recv[m], feat, n_tail)


def scatter_kernel(feat, n_tail, n_out, own, *refs):
    total = own[...]
    msgs, outs = refs[: -n_out], refs[-n_out:]
    for ref in msgs:
        total = total + decode(ref, feat, n_tail)
    q = encode(total, feat, n_tail)
    for ref in outs:
        ref[...] = q


def tree_kernel(feat, n_tail, order, *refs):
    n_in = len(order) + 1
    parts = [decode(refs[i], feat, n_tail) for i in [n_in - 1] + [order.index(m) for m in range(len(order))]]
    while len(parts) > 1:
        parts = [a + b for a, b in zip(parts[::2], parts[1::2])]
    q = encode(parts[0], feat, n_tail)
    for ref in refs[n_in:]:
        ref[...] = q


def unpack_kernel(feat, n_tail, classes, info, *refs):
    pieces, (g_in, b_in, g_out, b_out) = refs[:-4], refs[-4:]
    lanes = pieces[0].shape[1]
    half = len(pieces) // 2
    body = pieces[0].shape[0] - 2 * TAIL
    for c in range(2):
        for i, m in enumerate((0,) + (3, 1, 2)):
            at = (info[2] ^ c) * half + (info[1] ^ m)
            x = decode(pieces[c * half + i], feat, n_tail)
            where = pl.ds(pl.multiple_of(at * lanes, lanes), lanes)
            g_in[:, where] = x[:feat]
            g_out[:, where] = x[feat : feat + classes]
            b_in[:, where] = x[body : body + 1]

            @pl.when(at == 0)
            def _():
                for j in range(n_tail - 1):
                    b_out[:, j * lanes : (j + 1) * lanes] = x[body + 1 + j : body + 2 + j]


def xor_permute(x, axis, mask):
    return lax.ppermute(x, axis, [(i, i ^ mask) for i in range(lax.axis_size(axis))])


def swap_all(blocks):
    return [xor_permute(x, "dom", k) for k, x in zip(partners(len(blocks) + 1), blocks)]


def bit_groups(axis, first):
    size, bit, groups = lax.axis_size(axis), first, []
    while (1 << bit) < size:
        groups.append([m << bit for m in (1, 2, 3) if (m << bit) < size])
        bit += 2
    return groups


def reduce_grads(keep, recv, info, feat, n_tail, classes, hidden):
    count, rows, lanes = keep.shape
    coded = like((rows + TAIL, lanes), I16)
    own, *msgs = call(
        functools.partial(pair_kernel, feat, n_tail),
        [like((rows, lanes), F32)] + [coded] * (count - 1),
        [keep, recv],
    )
    msgs = [xor_permute(x, "dp", m + 1) for m, x in enumerate(msgs)]
    groups = [("dom", masks) for masks in bit_groups("dom", 1)] + [("dp", masks) for masks in bit_groups("dp", 2)]
    qs = call(functools.partial(scatter_kernel, feat, n_tail, 4), [coded] * 4, [own] + msgs)
    for axis, masks in groups:
        order = [m for m in (1, 0, 2) if m < len(masks)]
        got = [xor_permute(qs[i + 1], axis, masks[m]) for i, m in enumerate(order)]
        qs = call(functools.partial(tree_kernel, feat, n_tail, order), [coded] * 4, got + [qs[0]])
    pieces = [qs[0]] + [xor_permute(qs[i + 1], "dp", m) for i, m in enumerate((3, 1, 2))]
    pieces = pieces + [xor_permute(x, "dom", 1) for x in pieces]
    return call(
        functools.partial(unpack_kernel, feat, n_tail, classes),
        [like((feat, hidden), F32), like((1, hidden), F32), like((classes, hidden), F32), like((1, (n_tail - 1) * lanes), F32)],
        [info] + pieces,
        n_smem=1,
    )


def per_device(
    features,
    keep_masks,
    serve_ids,
    col_slot,
    adj_blocks,
    node_labels,
    labeled,
    weight_in,
    bias_in,
    weight_out,
    bias_out,
):
    tiles, nnz = col_slot.shape[1:]
    tile = adj_blocks.shape[-1]
    feat = features.shape[-1]
    samples = keep_masks.shape[1]
    hidden, classes = weight_out.shape
    dom = lax.axis_size("dom")
    me = lax.axis_index("dom")
    place = jnp.stack([me, lax.axis_index("dp") & 3, me & 1]).astype(I32)
    info = jnp.concatenate([place, serve_ids.reshape(-1)])
    adj = adj_blocks[0]
    feats = features.reshape(tiles, tile, feat)
    masks = keep_masks[0]
    lanes = samples * feat
    wide = -(-classes // 128) * 128

    rows = jnp.pad(masks.reshape(samples, tiles, tile).transpose(1, 0, 2), ((0, 0), (0, 16 - samples), (0, 0)))
    both = jnp.concatenate([feats, rows], 1)
    *msgs, both = call(
        select_kernel, [like((tile + 16, feat), BF16)] * (dom - 1) + [like(both.shape, BF16)], [info, both], n_smem=1
    )
    lhs, own, slots = call(
        functools.partial(layout_kernel, samples),
        [like((tiles, tile, nnz * tile), BF16), like((tiles, tile, lanes), BF16), like((tiles, nnz), I32)],
        [both, adj, col_slot[0]],
    )
    msgs = [xor_permute(x, "dom", k) for k, x in zip(partners_1(dom), msgs)]
    cur, total, *outs = call(
        functools.partial(hop1_kernel, dom, samples),
        [like((tiles, tile, lanes), BF16), like((tiles, tile, lanes), F32)] + [like((tile, lanes), BF16)] * (dom - 1),
        [info, slots, lhs, own] + msgs,
        [pltpu.VMEM((dom - 1 + tiles, tile, lanes), BF16)],
        n_smem=2,
    )
    late = min(LATE, dom - 2)
    half_w, half_b, w_out, half_w_t, b_out, code, outs[late] = call(
        prepare_kernel,
        [
            like((feat, hidden), BF16),
            like((1, hidden), F32),
            like((hidden, wide), BF16),
            like((wide, hidden), BF16),
            like((1, wide), F32),
            like((tile, -(-tiles // 8) * 8), I32),
            like(outs[late].shape, BF16),
        ],
        [weight_in, bias_in.reshape(1, hidden), weight_out.T, bias_out.reshape(1, classes)]
        + [node_labels.reshape(tiles, tile), labeled.reshape(tiles, tile), outs[late]],
    )
    outs = swap_all(outs)
    rows = samples * tile * tiles
    wide_t = -(-classes // 16) * 16
    half = like((hidden // 256, feat + wide_t + TAIL, 128), F32)
    send, *held = call(
        functools.partial(mlp_kernel, dom, samples, 1.0 / (samples * tiles * tile)),
        [
            half,
            like((feat, rows), BF16),
            like((rows, hidden), BF16),
            like((wide_t, rows), BF16),
            like((rows, hidden), BF16),
            like((8, hidden), F32),
            like((8, wide), F32),
        ],
        [info, slots, lhs, cur, total, code, half_w, half_b, w_out, half_w_t, b_out] + outs,
        [
            pltpu.VMEM((dom - 1 + tiles, tile, lanes), BF16),
            pltpu.VMEM((rows, hidden), F32),
            pltpu.VMEM((rows, wide), F32),
            pltpu.VMEM((rows, wide), BF16),
        ],
        n_smem=2,
        vmem=24,
    )
    recv = xor_permute(send, "dom", 1)
    keep = call(keep_kernel, half, [info] + held, n_smem=1)
    g_in, b_in, g_out, b_out = reduce_grads(keep, recv, info, feat, 1 + wide // 128, classes, hidden)
    return g_in, b_in.reshape(hidden), g_out.T, b_out.reshape(-1)[:classes]


def solution(mesh):
    placed = (
        P("dp", "dom", None),
        P("dp", None, "dom"),
        P("dp", "dom", None, None),
        P("dp", "dom", None),
        P("dp", "dom", None, None, None),
        P("dp", "dom"),
        P("dp", "dom"),
        P(),
        P(),
        P(),
        P(),
    )
    return jax.shard_map(
        per_device, mesh=mesh, in_specs=placed, out_specs=(P(), P(), P(), P()), check_vma=False
    )
```
